768 devices in a mesh: emb: 32 (over y_hi, x, core), dense: 24 (over z, y_lo).
Axes of the slice: x: 4, y: 8 (y_hi: 4, y_lo: 2; y = y_hi * 2 + y_lo), z: 12, core: 2. Of those that a mesh axis runs over, the one named last changes fastest.
Arguments:
- pooled: bfloat16 [18432, 3328], P('dense'), may hold values from -6 to 6
- upstream: bfloat16 [18432, 4096], P('dense', 'emb'), may hold values from -6 to 6
- preact: bfloat16 [18432, 4096], P('dense', 'emb'), may hold values from -6 to 6
- tower_w: bfloat16 [3328, 4096], P(None, 'emb'), may hold values from -0.109375 to 0.109375
- row_ids: int32 [18432, 26], P('dense'), may hold values from 0 to 65535, as said below
- table: float32 [65536, 128], P('emb'), may hold values from -4 to 4
- accum: float32 [65536], P('emb'), may hold values from 0.01 to 1
Outputs:
- weight_grad: float32 [3328, 4096], P(None, 'emb')
- bias_grad: float32 [4096], P('emb')
- new_table: float32 [65536, 128], P('emb')
- new_accum: float32 [65536], P('emb')
The draws below stay inside these ranges and needn't reach their ends.
Inputs may be any that keep to these rules, and one draw needn't show every extreme that they name: `row_ids`: row r is owned by index r // 2048 of emb. In each aligned block of 24 samples (the samples of one device, taken in order with dense as the slower index), at most 40 of the block's entries name rows of any one owner, and exactly 40 name rows of some owner.
All inputs are finite; a program needn't handle non-finite values.
Results may differ from the reference program's by a relative error of at most 0.007.
Values sent between devices are 32-bit elements; how exact they have to be, the bound alone decides.
A program may use at most 64 MiB of HBM per device.

```python
import math
import jax
import jax.numpy as jnp
from jax import lax

F = 26
E = 128
H = 4096
B_E = 24
ROWS_DEV = 2048
BATCH = 18432
K = 3328
V = 65536
CAP = 40
N_EMB = 32
N_DENSE = 24


def draw_row_ids(key, part):
    key = jax.random.fold_in(key, 11)
    entries = B_E * F
    blocks = N_EMB * N_DENSE

    def one_block(block_key):
        key_hot, key_slots, key_mix, key_rows = jax.random.split(block_key, 4)
        hot = jax.random.randint(key_hot, (), 0, N_EMB)
        others = jnp.arange((N_EMB - 1) * CAP, dtype=jnp.int32) // CAP
        others = others + (others >= hot).astype(jnp.int32)
        others = jax.random.permutation(key_slots, others)
        owners = jnp.concatenate([jnp.full((CAP,), hot, jnp.int32), others[:entries - CAP]])
        owners = jax.random.permutation(key_mix, owners)
        local = jnp.min(jax.random.randint(key_rows, (3, entries), 0, ROWS_DEV), axis=0)
        return (owners * ROWS_DEV + local).reshape(B_E, F)
    result = jax.vmap(one_block)(jax.random.split(key, blocks))
    return result.reshape(BATCH, F).astype(jnp.int32)


def level_of(rng, dims, cuts, smallest, largest):
    def one(axis_at, parts):
        heights = jax.random.uniform(jax.random.fold_in(jax.random.fold_in(rng, 6), axis_at), (parts,), jnp.float32, smallest / len(cuts), largest / len(cuts))
        return jnp.repeat(jnp.exp(heights), dims[axis_at] // parts).reshape((-1,) + (1,) * (len(dims) - axis_at - 1))

    gain = one(*cuts[0])
    for cut in cuts[1:]:
        gain = gain * one(*cut)
    return gain


def normal_values(rng, extent, spread, bound, shards=(), kind=jnp.bfloat16):
    factor_of = level_of(rng, extent, shards, -0.22, 0.18) if shards else 1.0
    array = jax.random.normal(rng, extent, jnp.float32) * spread * factor_of
    return jnp.minimum(jnp.maximum(array, -bound), bound).astype(kind)


def setup_inputs(seed: int = 0) -> dict:
    keys = jax.random.split(jax.random.key(seed), 8)
    pooled = normal_values(keys[0], (BATCH, K), 1.0, 6.0, ((0, 24),))
    upstream = normal_values(keys[1], (BATCH, H), 1.0, 6.0, ((0, 24), (1, 32)))
    preact = normal_values(keys[2], (BATCH, H), 1.5, 6.0, ((0, 24), (1, 32)))
    tower_w = normal_values(keys[3], (K, H), K ** -0.5, 0.109375, ((1, 32),))
    row_ids = draw_row_ids(jax.random.fold_in(keys[7], 71), 0)
    table = normal_values(keys[5], (V, E), 0.5, 4.0, ((0, 32),), jnp.float32)
    accum = jnp.clip(jnp.exp(math.log(1.0) - 4.6051702 * jax.random.uniform(keys[6], (V,), jnp.float32) ** level_of(keys[6], (V,), ((0, 32),), -0.2, 0.2)), 0.01, 1.0)
    return {"pooled": pooled, "upstream": upstream, "preact": preact, "tower_w": tower_w, "row_ids": row_ids, "table": table, "accum": accum}


learn_rate = 0.5

def reference(pooled, upstream, preact, tower_w, row_ids, table, accum):
    preact_f = preact.astype(jnp.float32)
    sigmoid_val = jax.nn.sigmoid(preact_f)
    slope = sigmoid_val * (1.0 + preact_f * (1.0 - sigmoid_val))
    deltas = (upstream.astype(jnp.float32) * slope).astype(jnp.bfloat16)
    weight_grad = jnp.dot(pooled.T, deltas, preferred_element_type=jnp.float32)
    bias_grad = lax.optimization_barrier(jnp.sum(deltas.astype(jnp.float32), axis=0))
    pooled_grad = jnp.dot(deltas, tower_w.T, preferred_element_type=jnp.float32)
    row_grad = jax.ops.segment_sum(pooled_grad.reshape(-1, E), row_ids.reshape(-1), num_segments=V)
    new_accum = accum + lax.optimization_barrier(jnp.mean(row_grad * row_grad, axis=1))
    new_table = table - learn_rate * row_grad / jnp.sqrt(new_accum)[:, None]
    return (weight_grad, bias_grad, new_table, new_accum)
```

```python
import functools

import jax
import jax.numpy as jnp
from jax import lax
from jax.experimental import pallas as pl
from jax.experimental.pallas import tpu as pltpu
from jax.sharding import PartitionSpec as P

learn_rate = 0.5
MESH = pl.DeviceIdType.MESH
CHUNK = 256
CAP = 40
F32 = jnp.float32
BF16 = jnp.bfloat16


def silu_slope(preact_f):
    sigmoid_val = jax.nn.sigmoid(preact_f)
    return sigmoid_val * (1.0 + preact_f * (1.0 - sigmoid_val))


def remote(src, dst, send, recv, where):
    return pltpu.make_async_remote_copy(
        src_ref=src, dst_ref=dst, send_sem=send, recv_sem=recv, device_id=where, device_id_type=MESH
    )


def place_rows(ids, groups, local_rows):
    entries = ids.shape[1]
    owners = ids // local_rows
    member = (lax.broadcasted_iota(jnp.int32, (groups, entries), 0) == owners).astype(F32)
    earlier = (
        lax.broadcasted_iota(jnp.int32, (entries, entries), 0)
        < lax.broadcasted_iota(jnp.int32, (entries, entries), 1)
    ).astype(F32).astype(BF16)
    prior = jnp.dot(member.astype(BF16), earlier, preferred_element_type=F32)
    ranks = jnp.sum(prior * member, axis=0, keepdims=True).astype(jnp.int32)
    slot_of = owners * CAP + ranks
    return (
        (lax.broadcasted_iota(jnp.int32, (groups * CAP, entries), 0) == slot_of)
        .astype(F32)
        .astype(BF16)
    )


def halves(rows):
    high = rows.astype(BF16)
    low = (rows - high.astype(F32)).astype(BF16)
    return jnp.concatenate([high, low], axis=1)


def route_kernel(
    ny,
    nx,
    local_rows,
    deltas_ref,
    w_ref,
    ids_ref,
    got_ref,
    spread,
    give,
    take,
    w_give,
    w_take,
    left,
    right,
    part,
    relay,
    from_x,
    from_y,
    grads,
    placing,
    out_rows,
    in_rows,
    pair_send,
    pair_recv,
    w_send,
    w_recv,
    x_send,
    x_recv,
    y_send,
    y_recv,
    a_send,
    a_recv,
):
    chunks = part.shape[0]
    batch = deltas_ref.shape[0] // (ny * nx * 2)
    groups = ny * nx * 2
    me = lax.axis_index("emb")
    core = lax.rem(me, 2)
    at_x = lax.rem(me // 2, nx)
    at_y = me // (2 * nx)

    def there(y, x, c):
        return {"emb": (lax.rem(y, ny) * nx + lax.rem(x, nx)) * 2 + c}

    sibling = there(at_y, at_x, 1 - core)
    x_next = there(at_y, at_x + 1, core)
    x_prev = there(at_y, at_x + nx - 1, core)
    y_next = there(at_y + 1, at_x, core)
    y_prev = there(at_y + ny - 1, at_x, core)
    y_far = there(at_y + 2, at_x, core)

    barrier = pltpu.get_barrier_semaphore()

    def greet(k, carry):
        pl.semaphore_signal(
            barrier, inc=1, device_id={"emb": lax.rem(me + k, groups)}, device_id_type=MESH
        )
        return carry

    lax.fori_loop(1, groups, greet, 0)

    spread[...] = deltas_ref[...].astype(F32).reshape(groups, batch, 128)
    for q in range(nx):
        for p in range(ny):
            block = (lax.rem(at_y + p, ny) * nx + lax.rem(at_x + q, nx)) * 2
            give[q * ny + p] = spread[block + 1 - core]
            left[pl.ds((q * ny + p) * batch, batch), :] = spread[block + core]
    w_give[...] = w_ref[...].astype(F32).reshape(w_give.shape)
    right[:, :, :128] = w_ref[...].reshape(chunks, CHUNK, 128)
    pl.semaphore_wait(barrier, groups - 1)

    def pair_copy():
        return remote(give, take, pair_send, pair_recv, sibling)

    def w_copy(j):
        return remote(w_give.at[j], w_take.at[j], w_send.at[j], w_recv.at[j], sibling)

    half = 2 * batch

    def x_copy(j, kind):
        if kind == 0:
            src, dst, where = part.at[j, 2, pl.ds(0, half)], relay.at[j, 0], x_next
        elif kind == 1:
            src, dst, where = part.at[j, 2, pl.ds(half, half)], relay.at[j, 1], x_prev
        elif kind == 2:
            src, dst, where = part.at[j, 1], from_x.at[j, 0], x_next
        else:
            src, dst, where = part.at[j, 3], from_x.at[j, 1], x_prev
        return remote(src, dst, x_send.at[kind, j], x_recv.at[kind, j], where)

    def y_copy(j, kind):
        where = (y_next, y_far, y_prev)[kind]
        src = part.at[j, 0, pl.ds((kind + 1) * batch, batch)]
        return remote(src, from_y.at[j, kind], y_send.at[kind, j], y_recv.at[kind, j], where)

    pair_copy().start()

    def w_start(j, carry):
        w_copy(j).start()
        return carry

    lax.fori_loop(0, chunks, w_start, 0)
    pair_copy().wait_recv()
    left_own = left[...].astype(BF16)
    left_pair = take[...].reshape(left.shape).astype(BF16)

    def step(i, carry):
        @pl.when(i < chunks)
        def _():
            w_copy(i).wait_recv()
            right[i, :, 128:] = w_take[i].astype(BF16)
            product = lax.dot_general(
                jnp.concatenate([left_own, left_pair], axis=1),
                right[i],
                (((1,), (1,)), ((), ())),
                preferred_element_type=F32,
            )
            part[i] = product.reshape(part.shape[1:])
            x_copy(i, 0).start()
            x_copy(i, 1).start()

        @pl.when(jnp.logical_and(i >= 2, i < chunks + 2))
        def _():
            j = i - 2
            x_copy(j, 0).wait_recv()
            part[j, 1, pl.ds(0, half)] = part[j, 1, pl.ds(0, half)] + relay[j, 0]
            x_copy(j, 2).start()
            x_copy(j, 1).wait_recv()
            part[j, 3, pl.ds(half, half)] = part[j, 3, pl.ds(half, half)] + relay[j, 1]
            x_copy(j, 3).start()

        @pl.when(i == 3)
        def _():
            placing[...] = place_rows(ids_ref[...], groups, local_rows)

        @pl.when(jnp.logical_and(i >= 4, i < chunks + 4))
        def _():
            j = i - 4
            x_copy(j, 2).wait_recv()
            x_copy(j, 3).wait_recv()
            part[j, 0] = part[j, 0] + from_x[j, 0] + from_x[j, 1]
            for kind in (1, 0, 2):
                y_copy(j, kind).start()

        @pl.when(i >= 7)
        def _():
            j = i - 7
            for kind in range(3):
                y_copy(j, kind).wait_recv()
            total = part[j, 0, pl.ds(0, batch)] + from_y[j, 0] + from_y[j, 1] + from_y[j, 2]
            for n in range(CHUNK // 128):
                grads[j * (CHUNK // 128) + n] = total[:, n * 128 : (n + 1) * 128]

        return carry

    lax.fori_loop(0, chunks + 7, step, 0)

    wide = halves(grads[...].reshape(-1, 128))
    both = jnp.dot(placing[...], wide, preferred_element_type=F32)
    out_rows[...] = (both[:, :128] + both[:, 128:]).reshape(out_rows.shape)

    def a_copy(k):
        owner = lax.rem(me + k, groups)
        return remote(
            out_rows.at[owner], in_rows.at[me], a_send.at[k], a_recv.at[k], {"emb": owner}
        )

    def a_start(k, carry):
        a_copy(lax.rem(k + 14, groups - 1) + 1).start()
        return carry

    lax.fori_loop(1, groups, a_start, 0)
    in_rows[me] = out_rows[me]

    def drain(j, carry):
        w_copy(j).wait_send()
        for kind in range(4):
            x_copy(j, kind).wait_send()
        for kind in range(3):
            y_copy(j, kind).wait_send()
        return carry

    pair_copy().wait_send()
    lax.fori_loop(0, chunks, drain, 0)

    def a_wait(k, carry):
        a_copy(k).wait_recv()
        a_copy(k).wait_send()
        return carry

    lax.fori_loop(1, groups, a_wait, 0)
    got_ref[...] = in_rows[...]


def route(deltas, tower_w, block_ids, local_rows, ny, nx):
    samples = deltas.shape[0]
    groups = ny * nx * 2
    batch = samples // groups
    columns = tower_w.shape[0]
    chunks = columns // CHUNK
    entries = block_ids.shape[1]
    vmem = pltpu.VMEM
    dma = pltpu.SemaphoreType.DMA
    return pl.pallas_call(
        functools.partial(route_kernel, ny, nx, local_rows),
        out_shape=jax.ShapeDtypeStruct((groups, CAP, 128), F32),
        in_specs=[pl.BlockSpec(memory_space=vmem)] * 3,
        out_specs=pl.BlockSpec(memory_space=vmem),
        scratch_shapes=[
            vmem((groups, batch, 128), F32),
            vmem((nx * ny, batch, 128), F32),
            vmem((nx * ny, batch, 128), F32),
            vmem((chunks, CHUNK, 128), F32),
            vmem((chunks, CHUNK, 128), F32),
            vmem((nx * ny * batch, 128), F32),
            vmem((chunks, CHUNK, 256), BF16),
            vmem((chunks, nx, ny * batch, CHUNK), F32),
            vmem((chunks, 2, 2 * batch, CHUNK), F32),
            vmem((chunks, 2, ny * batch, CHUNK), F32),
            vmem((chunks, 3, batch, CHUNK), F32),
            vmem((columns // 128, batch, 128), F32),
            vmem((groups * CAP, entries), BF16),
            vmem((groups, CAP, 128), F32),
            vmem((groups, CAP, 128), F32),
            dma,
            dma,
            dma((chunks,)),
            dma((chunks,)),
            dma((4, chunks)),
            dma((4, chunks)),
            dma((3, chunks)),
            dma((3, chunks)),
            dma((groups,)),
            dma((groups,)),
        ],
        compiler_params=pltpu.CompilerParams(
            collective_id=0, has_side_effects=True, vmem_limit_bytes=44 << 20
        ),
        cost_estimate=pl.CostEstimate(flops=1 << 30, bytes_accessed=8 << 20, transcendentals=0),
    )(deltas, tower_w, block_ids)


def landing_rows(ids, mine, local_rows):
    blocks, entries = ids.shape
    owners = ids // local_rows
    member = (owners == mine).astype(F32)
    earlier = (
        lax.broadcasted_iota(jnp.int32, (entries, entries), 0)
        < lax.broadcasted_iota(jnp.int32, (entries, entries), 1)
    ).astype(F32).astype(BF16)
    prior = jnp.dot(member.astype(BF16), earlier, preferred_element_type=F32)
    ranks = jnp.where(member > 0.5, prior.astype(jnp.int32), -1)
    offsets = (ids - owners * local_rows + 1).astype(F32)
    slots = lax.broadcasted_iota(jnp.int32, (CAP, entries), 0)
    columns = []
    for block in range(blocks):
        hit = jnp.where(slots == ranks[block : block + 1], offsets[block : block + 1], 0.0)
        columns.append(jnp.sum(hit, axis=1, keepdims=True))
    return jnp.concatenate(columns, axis=0) - 1.0


def update_kernel(
    nz,
    local_rows,
    rows_ref,
    ids_ref,
    bias_ref,
    total_ref,
    landing,
    sums,
    swap,
    mixed,
    from_z,
    final,
    s_send,
    s_recv,
    z_send,
    z_recv,
    g_send,
    g_recv,
    f_send,
    f_recv,
):
    mine = lax.axis_index("emb")
    me = lax.axis_index("dense")
    at_y = lax.rem(me, 2)
    at_z = me // 2
    shard = sums.shape[1]
    partner = {"dense": at_z * 2 + 1 - at_y}

    def away(k):
        return lax.rem(at_z + k, nz)

    def peer(k):
        return {"dense": away(k) * 2 + at_y}

    barrier = pltpu.get_barrier_semaphore()

    def greet(k, carry):
        pl.semaphore_signal(barrier, inc=1, device_id=peer(k), device_id_type=MESH)
        return carry

    lax.fori_loop(1, nz, greet, 0)
    pl.semaphore_signal(barrier, inc=1, device_id=partner, device_id_type=MESH)

    slots = rows_ref.shape[0] * rows_ref.shape[1]
    target = jnp.broadcast_to(landing_rows(ids_ref[...], mine, local_rows), (slots, 128))
    target = target.T[0:1].astype(jnp.int32)
    landing[...] = (
        (lax.broadcasted_iota(jnp.int32, (local_rows, slots), 0) == target)
        .astype(F32)
        .astype(BF16)
    )
    wide = halves(rows_ref[...].reshape(slots, 128))
    both = jnp.dot(landing[...], wide, preferred_element_type=F32)
    row_grad = both[:, :128] + both[:, 128:]
    spare = 2 * nz * shard - local_rows
    extra = jnp.where(
        lax.broadcasted_iota(jnp.int32, (spare, 128), 0) == 0,
        jnp.broadcast_to(bias_ref[...], (spare, 128)),
        0.0,
    )
    row_grad = jnp.concatenate([row_grad, extra], axis=0)
    sums[...] = row_grad.reshape(sums.shape)
    pl.semaphore_wait(barrier, nz)

    def s_copy(k):
        return remote(
            sums.at[away(k) * 2 + 1 - at_y], swap.at[k], s_send.at[k], s_recv.at[k], partner
        )

    def z_copy(k):
        return remote(mixed.at[k], from_z.at[k], z_send.at[k], z_recv.at[k], peer(k))

    def g_copy(k):
        return remote(final.at[me], final.at[me], g_send.at[k], g_recv.at[k], peer(k))

    def f_copy(k):
        source = away(nz - k) * 2 + at_y
        return remote(final.at[source], final.at[source], f_send.at[k], f_recv.at[k], partner)

    order = sorted(range(nz), key=lambda k: -min(k, nz - k))
    for k in order:
        s_copy(k).start()
    for k in order:
        s_copy(k).wait_recv()
        mixed[k] = sums[away(k) * 2 + at_y] + swap[k]
        if k:
            z_copy(k).start()
    total = mixed[0]
    for k in order[::-1]:
        if k:
            z_copy(k).wait_recv()
            total = total + from_z[k]
    final[me] = total
    for k in order:
        if k:
            g_copy(k).start()
    f_copy(0).start()
    for k in order[::-1]:
        if k:
            g_copy(k).wait_recv()
            f_copy(k).start()
    for k in order[::-1]:
        f_copy(k).wait_recv()
    for k in order:
        s_copy(k).wait_send()
        f_copy(k).wait_send()
        if k:
            z_copy(k).wait_send()
            g_copy(k).wait_send()
    total_ref[...] = final[...]


def update(rows, ids, bias, local_rows, dense):
    nz = dense // 2
    groups = rows.shape[0]
    shard = -(-(local_rows + 8) // (dense * 8)) * 8
    vmem = pltpu.VMEM
    dma = pltpu.SemaphoreType.DMA
    total = pl.pallas_call(
        functools.partial(update_kernel, nz, local_rows),
        out_shape=jax.ShapeDtypeStruct((dense, shard, 128), F32),
        in_specs=[pl.BlockSpec(memory_space=vmem)] * 3,
        out_specs=pl.BlockSpec(memory_space=vmem),
        scratch_shapes=[
            vmem((local_rows, groups * CAP), BF16),
            vmem((dense, shard, 128), F32),
            vmem((nz, shard, 128), F32),
            vmem((nz, shard, 128), F32),
            vmem((nz, shard, 128), F32),
            vmem((dense, shard, 128), F32),
        ]
        + [dma((nz,))] * 8,
        compiler_params=pltpu.CompilerParams(
            collective_id=1, has_side_effects=True, vmem_limit_bytes=44 << 20
        ),
        cost_estimate=pl.CostEstimate(flops=1 << 30, bytes_accessed=8 << 20, transcendentals=0),
    )(rows, ids, bias)
    return total.reshape(dense * shard, 128)


def shards(pooled, upstream, preact, tower_w, row_ids, table, accum):
    groups = lax.axis_size("emb")
    dense = lax.axis_size("dense")
    local_rows = table.shape[0]
    slope = silu_slope(preact.astype(F32))
    deltas = (upstream.astype(F32) * slope).astype(BF16)
    weight_grad = lax.dot_general(
        pooled, deltas, (((0,), (0,)), ((), ())), preferred_element_type=F32
    )
    bias = jnp.sum(deltas.astype(F32), axis=0)[None, :]
    weight_grad = lax.psum(weight_grad, "dense")
    ids = row_ids.reshape(groups, -1, row_ids.shape[1]).transpose(0, 2, 1).reshape(groups, -1)
    block_ids = lax.dynamic_slice_in_dim(ids, lax.axis_index("emb"), 1, 0)
    rows = route(deltas, tower_w, block_ids, local_rows, 4, 4)
    total = update(rows, ids, bias, local_rows, dense)
    row_grad = total[:local_rows]
    bias_grad = total[local_rows]
    new_accum = accum + jnp.mean(row_grad * row_grad, axis=1)
    new_table = table - learn_rate * row_grad / jnp.sqrt(new_accum)[:, None]
    return (weight_grad, bias_grad, new_table, new_accum)


def solution(mesh):
    placed = (
        P("dense", None),
        P("dense", "emb"),
        P("dense", "emb"),
        P(None, "emb"),
        P("dense", None),
        P("emb", None),
        P("emb"),
    )
    return jax.shard_map(
        shards,
        mesh=mesh,
        in_specs=placed,
        out_specs=(P(None, "emb"), P("emb"), P("emb", None), P("emb")),
        check_vma=False,
    )
```

```python
import functools

import jax
import jax.numpy as jnp
from jax import lax
from jax.experimental import pallas as pl
from jax.experimental.pallas import tpu as pltpu
from jax.sharding import PartitionSpec as P

learn_rate = 0.5
MESH = pl.DeviceIdType.MESH
CHUNK = 256
CAP = 40
F32 = jnp.float32
BF16 = jnp.bfloat16


def silu_slope(preact_f):
    sigmoid_val = jax.nn.sigmoid(preact_f)
    return sigmoid_val * (1.0 + preact_f * (1.0 - sigmoid_val))


def remote(src, dst, send, recv, where):
    return pltpu.make_async_remote_copy(
        src_ref=src, dst_ref=dst, send_sem=send, recv_sem=recv, device_id=where, device_id_type=MESH
    )


def place_rows(ids, groups, local_rows):
    entries = ids.shape[1]
    owners = ids // local_rows
    member = (lax.broadcasted_iota(jnp.int32, (groups, entries), 0) == owners).astype(F32)
    earlier = (
        lax.broadcasted_iota(jnp.int32, (entries, entries), 0)
        < lax.broadcasted_iota(jnp.int32, (entries, entries), 1)
    ).astype(F32).astype(BF16)
    prior = jnp.dot(member.astype(BF16), earlier, preferred_element_type=F32)
    ranks = jnp.sum(prior * member, axis=0, keepdims=True).astype(jnp.int32)
    slot_of = owners * CAP + ranks
    return (
        (lax.broadcasted_iota(jnp.int32, (groups * CAP, entries), 0) == slot_of)
        .astype(F32)
        .astype(BF16)
    )


def halves(rows):
    high = rows.astype(BF16)
    low = (rows - high.astype(F32)).astype(BF16)
    return jnp.concatenate([high, low], axis=1)


def landing_rows(ids, mine, local_rows):
    blocks, entries = ids.shape
    owners = ids // local_rows
    member = (owners == mine).astype(F32)
    earlier = (
        lax.broadcasted_iota(jnp.int32, (entries, entries), 0)
        < lax.broadcasted_iota(jnp.int32, (entries, entries), 1)
    ).astype(F32).astype(BF16)
    prior = jnp.dot(member.astype(BF16), earlier, preferred_element_type=F32)
    ranks = jnp.where(member > 0.5, prior.astype(jnp.int32), -1)
    offsets = (ids - owners * local_rows + 1).astype(F32)
    slots = lax.broadcasted_iota(jnp.int32, (CAP, entries), 0)
    columns = []
    for block in range(blocks):
        hit = jnp.where(slots == ranks[block : block + 1], offsets[block : block + 1], 0.0)
        columns.append(jnp.sum(hit, axis=1, keepdims=True))
    return jnp.concatenate(columns, axis=0) - 1.0


def step_kernel(
    ny,
    nx,
    nz,
    local_rows,
    deltas_ref,
    w_ref,
    mine_ref,
    ids_ref,
    wg_ref,
    bias_ref,
    total_ref,
    tower_ref,
    spread,
    give,
    take,
    w_give,
    w_take,
    left,
    right,
    part,
    relay,
    from_x,
    from_y,
    grads,
    placing,
    out_rows,
    in_rows,
    target,
    landing,
    sums,
    swap,
    mixed,
    from_z,
    final,
    tower,
    t_from,
    t_swap,
    t_final,
    pair_send,
    pair_recv,
    w_send,
    w_recv,
    x_send,
    x_recv,
    y_send,
    y_recv,
    a_send,
    a_recv,
    s_send,
    s_recv,
    z_send,
    z_recv,
    g_send,
    g_recv,
    f_send,
    f_recv,
    r_send,
    r_recv,
    b_send,
    b_recv,
    h_send,
    h_recv,
):
    chunks = part.shape[0]
    groups = ny * nx * 2
    batch = deltas_ref.shape[0] // groups
    columns = w_ref.shape[0]
    me = lax.axis_index("emb")
    core = lax.rem(me, 2)
    at_x = lax.rem(me // 2, nx)
    at_y = me // (2 * nx)
    replica = lax.axis_index("dense")
    at_low = lax.rem(replica, 2)
    at_z = replica // 2

    def there(y, x, c):
        return {"emb": (lax.rem(y, ny) * nx + lax.rem(x, nx)) * 2 + c}

    sibling = there(at_y, at_x, 1 - core)
    x_next = there(at_y, at_x + 1, core)
    x_prev = there(at_y, at_x + nx - 1, core)
    y_next = there(at_y + 1, at_x, core)
    y_prev = there(at_y + ny - 1, at_x, core)
    y_far = there(at_y + 2, at_x, core)
    partner = {"dense": at_z * 2 + 1 - at_low}

    def away(k):
        return lax.rem(at_z + k, nz)

    def peer(k):
        return {"dense": away(k) * 2 + at_low}

    z_ends = (peer(1), peer(nz - 1))

    barrier = pltpu.get_barrier_semaphore()

    def greet(k, carry):
        pl.semaphore_signal(
            barrier, inc=1, device_id={"emb": lax.rem(me + k, groups)}, device_id_type=MESH
        )
        return carry

    def greet_z(k, carry):
        pl.semaphore_signal(barrier, inc=1, device_id=peer(k), device_id_type=MESH)
        return carry

    lax.fori_loop(1, groups, greet, 0)
    lax.fori_loop(1, nz, greet_z, 0)
    pl.semaphore_signal(barrier, inc=1, device_id=partner, device_id_type=MESH)

    spread[...] = deltas_ref[...].astype(F32).reshape(groups, batch, 128)
    for q in range(nx):
        for p in range(ny):
            block = (lax.rem(at_y + p, ny) * nx + lax.rem(at_x + q, nx)) * 2
            give[q * ny + p] = spread[block + 1 - core]
            left[pl.ds((q * ny + p) * batch, batch), :] = spread[block + core]
    w_give[...] = w_ref[...].astype(F32).reshape(w_give.shape)
    right[:, :, :128] = w_ref[...].reshape(chunks, CHUNK, 128)

    part_rows = tower.shape[2]
    spare = nz * 2 * part_rows - columns
    extra = jnp.where(
        lax.broadcasted_iota(jnp.int32, (spare, 128), 0) == 0,
        jnp.broadcast_to(bias_ref[...], (spare, 128)),
        0.0,
    )
    tower[...] = jnp.concatenate([wg_ref[...], extra], axis=0).reshape(tower.shape)

    pl.semaphore_wait(barrier, groups - 1 + nz)

    turns = nz // 2
    bit = part_rows // 2

    def ring_at(way, k):
        return away(k) if way == 0 else away(nz - k)

    def r_copy(s, h, way):
        return remote(
            tower.at[ring_at(way, turns - s), h],
            t_from.at[way, s, h],
            r_send.at[way, s, h],
            r_recv.at[way, s, h],
            z_ends[way],
        )

    def r_first(h, way):
        rows = pl.ds(way * bit, bit)
        return remote(
            tower.at[away(turns), h, rows],
            t_from.at[way, 0, h, rows],
            r_send.at[way, 0, h],
            r_recv.at[way, 0, h],
            z_ends[way],
        )

    def b_copy(h):
        return remote(tower.at[at_z, h], t_swap.at[h], b_send.at[h], b_recv.at[h], partner)

    def h_copy(s, h, way):
        place = t_final.at[ring_at(1 - way, s), h]
        return remote(place, place, h_send.at[way, s, h], h_recv.at[way, s, h], z_ends[way])

    def h_last(h, way):
        place = t_final.at[ring_at(1 - way, turns - 1), h, pl.ds(way * bit, bit)]
        return remote(
            place,
            place,
            h_send.at[way, turns - 1, h],
            h_recv.at[way, turns - 1, h],
            z_ends[way],
        )

    def advance(n, carry):
        h = lax.rem(n, 2)
        s = n // 2

        @pl.when(s == 0)
        def _():
            for way in range(2):
                r_first(h, way).start()

        @pl.when(s == 1)
        def _():
            for way in range(2):
                r_first(h, way).wait_recv()
                t = ring_at(way, turns - 1)
                rows = pl.ds(way * bit, bit)
                tower[t, h, rows] = tower[t, h, rows] + t_from[way, 0, h, rows]
                r_copy(1, h, way).start()

        @pl.when(jnp.logical_and(s >= 2, s < turns))
        def _():
            for way in range(2):
                r_copy(s - 1, h, way).wait_recv()
                t = ring_at(way, turns - s)
                tower[t, h] = tower[t, h] + t_from[way, s - 1, h]
                r_copy(s, h, way).start()

        @pl.when(s == turns)
        def _():
            r_copy(turns - 1, h, 0).wait_recv()
            r_copy(turns - 1, h, 1).wait_recv()
            tower[at_z, h] = (
                tower[at_z, h] + t_from[0, turns - 1, h] + t_from[1, turns - 1, h]
            )
            b_copy(h).start()

        @pl.when(s == turns + 1)
        def _():
            b_copy(h).wait_recv()
            t_final[at_z, h] = tower[at_z, h] + t_swap[h]
            for way in range(2):
                h_copy(0, h, way).start()

        @pl.when(jnp.logical_and(s >= turns + 2, s < 2 * turns))
        def _():
            for way in range(2):
                h_copy(s - turns - 2, h, way).wait_recv()
                h_copy(s - turns - 1, h, way).start()

        @pl.when(s == 2 * turns)
        def _():
            for way in range(2):
                h_copy(turns - 2, h, way).wait_recv()
                h_last(h, way).start()

        @pl.when(s == 2 * turns + 1)
        def _():
            for way in range(2):
                h_last(h, way).wait_recv()

        return carry

    advances = 2 * (2 * turns + 2)

    def pair_copy():
        return remote(give, take, pair_send, pair_recv, sibling)

    def w_copy(j):
        return remote(w_give.at[j], w_take.at[j], w_send.at[j], w_recv.at[j], sibling)

    half = 2 * batch

    def x_copy(j, kind):
        if kind == 0:
            src, dst, where = part.at[j, 2, pl.ds(0, half)], relay.at[j, 0], x_next
        elif kind == 1:
            src, dst, where = part.at[j, 2, pl.ds(half, half)], relay.at[j, 1], x_prev
        elif kind == 2:
            src, dst, where = part.at[j, 1], from_x.at[j, 0], x_next
        else:
            src, dst, where = part.at[j, 3], from_x.at[j, 1], x_prev
        return remote(src, dst, x_send.at[kind, j], x_recv.at[kind, j], where)

    def y_copy(j, kind):
        where = (y_next, y_far, y_prev)[kind]
        src = part.at[j, 0, pl.ds((kind + 1) * batch, batch)]
        return remote(src, from_y.at[j, kind], y_send.at[kind, j], y_recv.at[kind, j], where)

    pair_copy().start()

    def w_start(j, carry):
        w_copy(j).start()
        return carry

    lax.fori_loop(0, chunks, w_start, 0)
    lax.fori_loop(0, 2, advance, 0)
    pair_copy().wait_recv()
    left_own = left[...].astype(BF16)
    left_pair = take[...].reshape(left.shape).astype(BF16)
    lead_s2, lead_y, lead_end = 3, 6, 9
    slots = groups * CAP
    slabs = 8
    slab = local_rows // slabs

    def first_advance(i):
        return jnp.minimum(2 + (4 * i) // 3, advances)

    def step(i, carry):
        @pl.when(i < chunks)
        def _():
            w_copy(i).wait_recv()
            right[i, :, 128:] = w_take[i].astype(BF16)
            product = lax.dot_general(
                jnp.concatenate([left_own, left_pair], axis=1),
                right[i],
                (((1,), (1,)), ((), ())),
                preferred_element_type=F32,
            )
            part[i] = product.reshape(part.shape[1:])
            x_copy(i, 0).start()
            x_copy(i, 1).start()

        @pl.when(jnp.logical_and(i >= lead_s2, i < chunks + lead_s2))
        def _():
            j = i - lead_s2
            x_copy(j, 0).wait_recv()
            part[j, 1, pl.ds(0, half)] = part[j, 1, pl.ds(0, half)] + relay[j, 0]
            x_copy(j, 2).start()
            x_copy(j, 1).wait_recv()
            part[j, 3, pl.ds(half, half)] = part[j, 3, pl.ds(half, half)] + relay[j, 1]
            x_copy(j, 3).start()

        lax.fori_loop(first_advance(i), first_advance(i + 1), advance, 0)

        @pl.when(i == 4)
        def _():
            placing[...] = place_rows(mine_ref[...], groups, local_rows)

        @pl.when(i == 6)
        def _():
            wide = jnp.broadcast_to(landing_rows(ids_ref[...], me, local_rows), (slots, 128))
            target[...] = wide.T[0:8].astype(jnp.int32)

        @pl.when(jnp.logical_and(i >= 7, i < 7 + slabs))
        def _():
            first = (i - 7) * slab
            rows = lax.broadcasted_iota(jnp.int32, (slab, slots), 0) + first
            landing[i - 7] = (rows == target[0:1]).astype(F32).astype(BF16)

        @pl.when(jnp.logical_and(i >= lead_y, i < chunks + lead_y))
        def _():
            j = i - lead_y
            x_copy(j, 2).wait_recv()
            x_copy(j, 3).wait_recv()
            part[j, 0] = part[j, 0] + from_x[j, 0] + from_x[j, 1]
            for kind in (1, 0, 2):
                y_copy(j, kind).start()

        @pl.when(i >= lead_end)
        def _():
            j = i - lead_end
            for kind in range(3):
                y_copy(j, kind).wait_recv()
            total = part[j, 0, pl.ds(0, batch)] + from_y[j, 0] + from_y[j, 1] + from_y[j, 2]
            for n in range(CHUNK // 128):
                grads[j * (CHUNK // 128) + n] = total[:, n * 128 : (n + 1) * 128]

        return carry

    lax.fori_loop(0, chunks + lead_end, step, 0)

    wide = halves(grads[...].reshape(-1, 128))
    both = jnp.dot(placing[...], wide, preferred_element_type=F32)
    out_rows[...] = (both[:, :128] + both[:, 128:]).reshape(out_rows.shape)

    def a_copy(k):
        owner = lax.rem(me + k, groups)
        return remote(
            out_rows.at[owner], in_rows.at[me], a_send.at[k], a_recv.at[k], {"emb": owner}
        )

    def a_start(k, carry):
        a_copy(lax.rem(k + 14, groups - 1) + 1).start()
        return carry

    lax.fori_loop(1, groups, a_start, 0)
    in_rows[me] = out_rows[me]
    lax.fori_loop(first_advance(chunks + lead_end), advances, advance, 0)

    def a_wait(k, carry):
        a_copy(k).wait_recv()
        return carry

    lax.fori_loop(1, groups, a_wait, 0)

    wide = halves(in_rows[...].reshape(slots, 128))
    both = jnp.dot(
        landing[...].reshape(local_rows, slots), wide, preferred_element_type=F32
    )
    row_grad = both[:, :128] + both[:, 128:]
    shard = sums.shape[1]
    unused = 2 * nz * shard - local_rows
    if unused:
        row_grad = jnp.concatenate([row_grad, jnp.zeros((unused, 128), F32)], axis=0)
    sums[...] = row_grad.reshape(sums.shape)

    def s_copy(k):
        return remote(
            sums.at[away(k) * 2 + 1 - at_low], swap.at[k], s_send.at[k], s_recv.at[k], partner
        )

    def z_copy(k):
        return remote(mixed.at[k], from_z.at[k], z_send.at[k], z_recv.at[k], peer(k))

    def g_copy(k):
        place = final.at[replica]
        return remote(place, place, g_send.at[k], g_recv.at[k], peer(k))

    def f_copy(k):
        place = final.at[away(nz - k) * 2 + at_low]
        return remote(place, place, f_send.at[k], f_recv.at[k], partner)

    order = sorted(range(nz), key=lambda k: -min(k, nz - k))
    for k in order:
        s_copy(k).start()
    for k in order:
        s_copy(k).wait_recv()
        mixed[k] = sums[away(k) * 2 + at_low] + swap[k]
        if k:
            z_copy(k).start()
    tower_ref[...] = t_final[...].reshape(nz * 2 * part_rows, 128)[: columns + 8]
    total = mixed[0]
    for k in order[::-1]:
        if k:
            z_copy(k).wait_recv()
            total = total + from_z[k]
    final[replica] = total
    for k in order:
        if k:
            g_copy(k).start()
    f_copy(0).start()

    def drain(j, carry):
        w_copy(j).wait_send()
        for kind in range(4):
            x_copy(j, kind).wait_send()
        for kind in range(3):
            y_copy(j, kind).wait_send()
        return carry

    def a_drain(k, carry):
        a_copy(k).wait_send()
        return carry

    def t_drain(h, carry):
        for way in range(2):
            r_first(h, way).wait_send()
            h_last(h, way).wait_send()
            h_copy(0, h, way).wait_send()
        b_copy(h).wait_send()

        def inner(s, carry):
            for way in range(2):
                r_copy(s, h, way).wait_send()
            return carry

        def inner_h(s, carry):
            for way in range(2):
                h_copy(s, h, way).wait_send()
            return carry

        lax.fori_loop(1, turns, inner, 0)
        lax.fori_loop(1, turns - 1, inner_h, 0)
        return carry

    pair_copy().wait_send()
    lax.fori_loop(0, chunks, drain, 0)
    lax.fori_loop(1, groups, a_drain, 0)
    lax.fori_loop(0, 2, t_drain, 0)
    for k in order[::-1]:
        if k:
            g_copy(k).wait_recv()
            f_copy(k).start()
    for k in order[::-1]:
        f_copy(k).wait_recv()
    for k in order:
        s_copy(k).wait_send()
        f_copy(k).wait_send()
        if k:
            z_copy(k).wait_send()
            g_copy(k).wait_send()
    total_ref[...] = final[...]


def step(deltas, tower_w, block_ids, ids, tower_grad, bias, local_rows, dense, ny, nx):
    samples = deltas.shape[0]
    groups = ny * nx * 2
    nz = dense // 2
    batch = samples // groups
    columns = tower_w.shape[0]
    chunks = columns // CHUNK
    entries = block_ids.shape[1]
    slots = groups * CAP
    shard = -(-local_rows // (dense * 8)) * 8
    piece = -(-(columns + 8) // (nz * 32)) * 16
    turns = nz // 2
    vmem = pltpu.VMEM
    dma = pltpu.SemaphoreType.DMA
    total, tower = pl.pallas_call(
        functools.partial(step_kernel, ny, nx, nz, local_rows),
        out_shape=(
            jax.ShapeDtypeStruct((dense, shard, 128), F32),
            jax.ShapeDtypeStruct((columns + 8, 128), F32),
        ),
        in_specs=[pl.BlockSpec(memory_space=vmem)] * 6,
        out_specs=[pl.BlockSpec(memory_space=vmem)] * 2,
        scratch_shapes=[
            vmem((groups, batch, 128), F32),
            vmem((nx * ny, batch, 128), F32),
            vmem((nx * ny, batch, 128), F32),
            vmem((chunks, CHUNK, 128), F32),
            vmem((chunks, CHUNK, 128), F32),
            vmem((nx * ny * batch, 128), F32),
            vmem((chunks, CHUNK, 256), BF16),
            vmem((chunks, nx, ny * batch, CHUNK), F32),
            vmem((chunks, 2, 2 * batch, CHUNK), F32),
            vmem((chunks, 2, ny * batch, CHUNK), F32),
            vmem((chunks, 3, batch, CHUNK), F32),
            vmem((columns // 128, batch, 128), F32),
            vmem((slots, entries), BF16),
            vmem((groups, CAP, 128), F32),
            vmem((groups, CAP, 128), F32),
            vmem((8, slots), jnp.int32),
            vmem((8, local_rows // 8, slots), BF16),
            vmem((dense, shard, 128), F32),
            vmem((nz, shard, 128), F32),
            vmem((nz, shard, 128), F32),
            vmem((nz, shard, 128), F32),
            vmem((dense, shard, 128), F32),
            vmem((nz, 2, piece, 128), F32),
            vmem((2, turns, 2, piece, 128), F32),
            vmem((2, piece, 128), F32),
            vmem((nz, 2, piece, 128), F32),
            dma,
            dma,
            dma((chunks,)),
            dma((chunks,)),
            dma((4, chunks)),
            dma((4, chunks)),
            dma((3, chunks)),
            dma((3, chunks)),
            dma((groups,)),
            dma((groups,)),
        ]
        + [dma((nz,))] * 8
        + [
            dma((2, turns, 2)),
            dma((2, turns, 2)),
            dma((2,)),
            dma((2,)),
            dma((2, turns, 2)),
            dma((2, turns, 2)),
        ],
        compiler_params=pltpu.CompilerParams(
            collective_id=0, has_side_effects=True, vmem_limit_bytes=58 << 20
        ),
        cost_estimate=pl.CostEstimate(flops=1 << 30, bytes_accessed=8 << 20, transcendentals=0),
    )(deltas, tower_w, block_ids, ids, tower_grad, bias)
    return total.reshape(dense * shard, 128), tower


def shards(pooled, upstream, preact, tower_w, row_ids, table, accum):
    groups = lax.axis_size("emb")
    dense = lax.axis_size("dense")
    local_rows = table.shape[0]
    slope = silu_slope(preact.astype(F32))
    deltas = (upstream.astype(F32) * slope).astype(BF16)
    weight_grad = lax.dot_general(
        pooled, deltas, (((0,), (0,)), ((), ())), preferred_element_type=F32
    )
    bias = jnp.sum(deltas.astype(F32), axis=0)[None, :]
    ids = row_ids.reshape(groups, -1, row_ids.shape[1]).transpose(0, 2, 1).reshape(groups, -1)
    block_ids = lax.dynamic_slice_in_dim(ids, lax.axis_index("emb"), 1, 0)
    total, tower = step(
        deltas, tower_w, block_ids, ids, weight_grad, bias, local_rows, dense, 4, 4
    )
    columns = tower_w.shape[0]
    row_grad = total[:local_rows]
    new_accum = accum + jnp.mean(row_grad * row_grad, axis=1)
    new_table = table - learn_rate * row_grad / jnp.sqrt(new_accum)[:, None]
    return (tower[:columns], tower[columns], new_table, new_accum)


def solution(mesh):
    placed = (
        P("dense", None),
        P("dense", "emb"),
        P("dense", "emb"),
        P(None, "emb"),
        P("dense", None),
        P("emb", None),
        P("emb"),
    )
    return jax.shard_map(
        shards,
        mesh=mesh,
        in_specs=placed,
        out_specs=(P(None, "emb"), P("emb"), P("emb", None), P("emb")),
        check_vma=False,
    )
```

```python
import functools

import jax
import jax.numpy as jnp
from jax import lax
from jax.experimental import pallas as pl
from jax.experimental.pallas import tpu as pltpu
from jax.sharding import PartitionSpec as P

learn_rate = 0.5
MESH = pl.DeviceIdType.MESH
CHUNK = 256
CAP = 40
F32 = jnp.float32
BF16 = jnp.bfloat16


def silu_slope(preact_f):
    sigmoid_val = jax.nn.sigmoid(preact_f)
    return sigmoid_val * (1.0 + preact_f * (1.0 - sigmoid_val))


def remote(src, dst, send, recv, where):
    return pltpu.make_async_remote_copy(
        src_ref=src, dst_ref=dst, send_sem=send, recv_sem=recv, device_id=where, device_id_type=MESH
    )


def place_rows(ids, groups, local_rows):
    entries = ids.shape[1]
    owners = ids // local_rows
    member = (lax.broadcasted_iota(jnp.int32, (groups, entries), 0) == owners).astype(F32)
    earlier = (
        lax.broadcasted_iota(jnp.int32, (entries, entries), 0)
        < lax.broadcasted_iota(jnp.int32, (entries, entries), 1)
    ).astype(F32).astype(BF16)
    prior = jnp.dot(member.astype(BF16), earlier, preferred_element_type=F32)
    ranks = jnp.sum(prior * member, axis=0, keepdims=True).astype(jnp.int32)
    slot_of = owners * CAP + ranks
    return (
        (lax.broadcasted_iota(jnp.int32, (groups * CAP, entries), 0) == slot_of)
        .astype(F32)
        .astype(BF16)
    )


def halves(rows):
    high = rows.astype(BF16)
    low = (rows - high.astype(F32)).astype(BF16)
    return jnp.concatenate([high, low], axis=1)


def landing_rows(ids, mine, local_rows):
    blocks, entries = ids.shape
    owners = ids // local_rows
    member = (owners == mine).astype(F32)
    earlier = (
        lax.broadcasted_iota(jnp.int32, (entries, entries), 0)
        < lax.broadcasted_iota(jnp.int32, (entries, entries), 1)
    ).astype(F32).astype(BF16)
    prior = jnp.dot(member.astype(BF16), earlier, preferred_element_type=F32)
    ranks = jnp.where(member > 0.5, prior.astype(jnp.int32), -1)
    offsets = (ids - owners * local_rows + 1).astype(F32)
    slots = lax.broadcasted_iota(jnp.int32, (CAP, entries), 0)
    columns = []
    for block in range(blocks):
        hit = jnp.where(slots == ranks[block : block + 1], offsets[block : block + 1], 0.0)
        columns.append(jnp.sum(hit, axis=1, keepdims=True))
    return jnp.concatenate(columns, axis=0) - 1.0


def step_kernel(
    ny,
    nx,
    nz,
    local_rows,
    pooled_ref,
    upstream_ref,
    preact_ref,
    w_ref,
    mine_ref,
    ids_ref,
    total_ref,
    tower_ref,
    pooled,
    spread,
    give,
    take,
    w_give,
    w_take,
    left,
    right,
    part,
    relay,
    from_x,
    from_y,
    grads,
    placing,
    out_rows,
    in_rows,
    target,
    landing,
    sums,
    swap,
    mixed,
    from_z,
    merge,
    final,
    tower,
    t_from,
    t_swap,
    t_final,
    pair_send,
    pair_recv,
    w_send,
    w_recv,
    x_send,
    x_recv,
    y_send,
    y_recv,
    a_send,
    a_recv,
    s_send,
    s_recv,
    z_send,
    z_recv,
    g_send,
    g_recv,
    f_send,
    f_recv,
    r_send,
    r_recv,
    b_send,
    b_recv,
    h_send,
    h_recv,
    q_send,
    q_recv,
    e_send,
    e_recv,
    in_sem,
    out_sem,
):
    chunks = part.shape[0]
    groups = ny * nx * 2
    batch = upstream_ref.shape[0] // groups
    columns = w_ref.shape[0]
    me = lax.axis_index("emb")
    core = lax.rem(me, 2)
    at_x = lax.rem(me // 2, nx)
    at_y = me // (2 * nx)
    replica = lax.axis_index("dense")
    at_low = lax.rem(replica, 2)
    at_z = replica // 2

    def there(y, x, c):
        return {"emb": (lax.rem(y, ny) * nx + lax.rem(x, nx)) * 2 + c}

    sibling = there(at_y, at_x, 1 - core)
    x_next = there(at_y, at_x + 1, core)
    x_prev = there(at_y, at_x + nx - 1, core)
    y_next = there(at_y + 1, at_x, core)
    y_prev = there(at_y + ny - 1, at_x, core)
    y_far = there(at_y + 2, at_x, core)
    partner = {"dense": at_z * 2 + 1 - at_low}

    def away(k):
        return lax.rem(at_z + k, nz)

    def peer(k):
        return {"dense": away(k) * 2 + at_low}

    z_ends = (peer(1), peer(nz - 1))

    load = pltpu.make_async_copy(pooled_ref, pooled, in_sem)
    load.start()
    barrier = pltpu.get_barrier_semaphore()

    def greet(k, carry):
        pl.semaphore_signal(
            barrier, inc=1, device_id={"emb": lax.rem(me + k, groups)}, device_id_type=MESH
        )
        return carry

    def greet_z(k, carry):
        pl.semaphore_signal(barrier, inc=1, device_id=peer(k), device_id_type=MESH)
        return carry

    lax.fori_loop(1, groups, greet, 0)
    lax.fori_loop(1, nz, greet_z, 0)
    pl.semaphore_signal(barrier, inc=1, device_id=partner, device_id_type=MESH)

    slope = silu_slope(preact_ref[...].astype(F32))
    deltas = (upstream_ref[...].astype(F32) * slope).astype(BF16).astype(F32)
    spread[...] = deltas.reshape(groups, batch, 128)
    for q in range(nx):
        for p in range(ny):
            block = (lax.rem(at_y + p, ny) * nx + lax.rem(at_x + q, nx)) * 2
            give[q * ny + p] = spread[block + 1 - core]
            left[pl.ds((q * ny + p) * batch, batch), :] = spread[block + core]
    w_give[...] = w_ref[...].astype(F32).reshape(w_give.shape)
    right[:, :, :128] = w_ref[...].reshape(chunks, CHUNK, 128)

    pl.semaphore_wait(barrier, groups - 1 + nz)

    turns = nz // 2
    part_rows = t_swap.shape[1]
    bit = part_rows // 2

    def stretch(t, h, first=0, size=part_rows):
        return pl.ds(pl.multiple_of((t * 2 + h) * part_rows + first, 8), size)

    def ring_at(way, k):
        return away(k) if way == 0 else away(nz - k)

    def r_copy(s, h, way):
        return remote(
            tower.at[stretch(ring_at(way, turns - s), h)],
            t_from.at[way, s, h],
            r_send.at[way, s, h],
            r_recv.at[way, s, h],
            z_ends[way],
        )

    def r_first(h, way):
        rows = pl.ds(way * bit, bit)
        return remote(
            tower.at[stretch(away(turns), h, way * bit, bit)],
            t_from.at[way, 0, h, rows],
            r_send.at[way, 0, h],
            r_recv.at[way, 0, h],
            z_ends[way],
        )

    def b_copy(h):
        place = tower.at[stretch(at_z, h)]
        return remote(place, t_swap.at[h], b_send.at[h], b_recv.at[h], partner)

    def h_copy(s, h, way):
        place = t_final.at[stretch(ring_at(1 - way, s), h)]
        return remote(place, place, h_send.at[way, s, h], h_recv.at[way, s, h], z_ends[way])

    def h_last(h, way):
        place = t_final.at[stretch(ring_at(1 - way, turns - 1), h, way * bit, bit)]
        return remote(
            place,
            place,
            h_send.at[way, turns - 1, h],
            h_recv.at[way, turns - 1, h],
            z_ends[way],
        )

    def advance(n, carry):
        h = lax.rem(n, 2)
        s = n // 2

        @pl.when(s == 0)
        def _():
            for way in range(2):
                r_first(h, way).start()

        @pl.when(s == 1)
        def _():
            for way in range(2):
                r_first(h, way).wait_recv()
                t = ring_at(way, turns - 1)
                rows = pl.ds(way * bit, bit)
                here = stretch(t, h, way * bit, bit)
                tower[here, :] = tower[here, :] + t_from[way, 0, h, rows]
                r_copy(1, h, way).start()

        @pl.when(jnp.logical_and(s >= 2, s < turns))
        def _():
            for way in range(2):
                r_copy(s - 1, h, way).wait_recv()
                t = ring_at(way, turns - s)
                tower[stretch(t, h), :] = tower[stretch(t, h), :] + t_from[way, s - 1, h]
                r_copy(s, h, way).start()

        @pl.when(s == turns)
        def _():
            r_copy(turns - 1, h, 0).wait_recv()
            r_copy(turns - 1, h, 1).wait_recv()
            here = stretch(at_z, h)
            tower[here, :] = (
                tower[here, :] + t_from[0, turns - 1, h] + t_from[1, turns - 1, h]
            )
            b_copy(h).start()

        @pl.when(s == turns + 1)
        def _():
            b_copy(h).wait_recv()
            t_final[stretch(at_z, h), :] = tower[stretch(at_z, h), :] + t_swap[h]
            for way in range(2):
                h_copy(0, h, way).start()

        @pl.when(jnp.logical_and(s >= turns + 2, s < 2 * turns))
        def _():
            for way in range(2):
                h_copy(s - turns - 2, h, way).wait_recv()
                h_copy(s - turns - 1, h, way).start()

        @pl.when(s == 2 * turns)
        def _():
            for way in range(2):
                h_copy(turns - 2, h, way).wait_recv()
                h_last(h, way).start()

        @pl.when(s == 2 * turns + 1)
        def _():
            for way in range(2):
                h_last(h, way).wait_recv()

        return carry

    advances = 2 * (2 * turns + 2)

    def pair_copy():
        return remote(give, take, pair_send, pair_recv, sibling)

    def w_copy(j):
        return remote(w_give.at[j], w_take.at[j], w_send.at[j], w_recv.at[j], sibling)

    half = 2 * batch

    def x_copy(j, kind):
        if kind == 0:
            src, dst, where = part.at[j, 2, pl.ds(0, half)], relay.at[j, 0], x_next
        elif kind == 1:
            src, dst, where = part.at[j, 2, pl.ds(half, half)], relay.at[j, 1], x_prev
        elif kind == 2:
            src, dst, where = part.at[j, 1], from_x.at[j, 0], x_next
        else:
            src, dst, where = part.at[j, 3], from_x.at[j, 1], x_prev
        return remote(src, dst, x_send.at[kind, j], x_recv.at[kind, j], where)

    def y_copy(j, kind):
        where = (y_next, y_far, y_prev)[kind]
        src = part.at[j, 0, pl.ds((kind + 1) * batch, batch)]
        return remote(src, from_y.at[j, kind], y_send.at[kind, j], y_recv.at[kind, j], where)

    pair_copy().start()

    def w_start(j, carry):
        w_copy(j).start()
        return carry

    lax.fori_loop(0, chunks, w_start, 0)
    pair_copy().wait_recv()
    left_own = left[...].astype(BF16)
    left_pair = take[...].reshape(left.shape).astype(BF16)
    ahead = 4
    lead_s2, lead_y, lead_end = ahead, ahead + 3, ahead + 6
    slots = groups * CAP
    shard = swap.shape[1]

    def first_advance(i):
        return jnp.minimum(2 + (3 * (i - ahead)) // 2, advances)

    def multiply(i, carry):
        w_copy(i).wait_recv()
        right[i, :, 128:] = w_take[i].astype(BF16)
        product = lax.dot_general(
            jnp.concatenate([left_own, left_pair], axis=1),
            right[i],
            (((1,), (1,)), ((), ())),
            preferred_element_type=F32,
        )
        part[i] = product.reshape(part.shape[1:])
        x_copy(i, 0).start()
        x_copy(i, 1).start()
        return carry

    lax.fori_loop(0, ahead, multiply, 0)

    spare = tower.shape[0] - columns
    every = spread[...].reshape(groups * batch, 128)
    tower[pl.ds(columns, spare), :] = jnp.where(
        lax.broadcasted_iota(jnp.int32, (spare, 128), 0) == 0,
        jnp.broadcast_to(jnp.sum(every, axis=0, keepdims=True), (spare, 128)),
        0.0,
    )
    turned = every.T.astype(BF16)
    load.wait()
    for j in range(chunks):
        flat = jnp.dot(
            turned, pooled[:, j * CHUNK : (j + 1) * CHUNK], preferred_element_type=F32
        )
        tower[j * CHUNK : (j + 1) * CHUNK, :] = flat.T
    lax.fori_loop(0, 2, advance, 0)

    def step(i, carry):
        @pl.when(i < chunks)
        def _():
            multiply(i, 0)

        @pl.when(jnp.logical_and(i >= lead_s2, i < chunks + lead_s2))
        def _():
            j = i - lead_s2
            x_copy(j, 0).wait_recv()
            part[j, 1, pl.ds(0, half)] = part[j, 1, pl.ds(0, half)] + relay[j, 0]
            x_copy(j, 2).start()
            x_copy(j, 1).wait_recv()
            part[j, 3, pl.ds(half, half)] = part[j, 3, pl.ds(half, half)] + relay[j, 1]
            x_copy(j, 3).start()

        lax.fori_loop(first_advance(i), first_advance(i + 1), advance, 0)

        @pl.when(i == 5)
        def _():
            placing[...] = place_rows(mine_ref[...], groups, local_rows)

        @pl.when(i == 6)
        def _():
            wide = jnp.broadcast_to(landing_rows(ids_ref[...], me, local_rows), (slots, 128))
            target[...] = wide.T[0:8].astype(jnp.int32)

        @pl.when(jnp.logical_and(i >= 7, i < 7 + nz))
        def _():
            n = i - 7
            k = turns + jnp.where(lax.rem(n, 2) == 0, (n + 1) // 2, -((n + 1) // 2))
            rows = lax.broadcasted_iota(jnp.int32, (shard, slots), 0)
            for low in range(2):
                owned = 1 - at_low if low == 0 else at_low
                hit = rows + (away(k) * 2 + owned) * shard == target[0:1]
                landing[n, pl.ds(low * shard, shard), :] = hit.astype(F32).astype(BF16)

        @pl.when(jnp.logical_and(i >= lead_y, i < chunks + lead_y))
        def _():
            j = i - lead_y
            x_copy(j, 2).wait_recv()
            x_copy(j, 3).wait_recv()
            part[j, 0] = part[j, 0] + from_x[j, 0] + from_x[j, 1]
            for kind in (1, 0, 2):
                y_copy(j, kind).start()

        @pl.when(i >= lead_end)
        def _():
            j = i - lead_end
            for kind in range(3):
                y_copy(j, kind).wait_recv()
            total = part[j, 0, pl.ds(0, batch)] + from_y[j, 0] + from_y[j, 1] + from_y[j, 2]
            for n in range(CHUNK // 128):
                grads[j * (CHUNK // 128) + n] = total[:, n * 128 : (n + 1) * 128]

        return carry

    lax.fori_loop(ahead, chunks + lead_end, step, 0)

    wide = halves(grads[...].reshape(-1, 128))
    both = jnp.dot(placing[...], wide, preferred_element_type=F32)
    out_rows[...] = (both[:, :128] + both[:, 128:]).reshape(out_rows.shape)

    def a_copy(k):
        owner = lax.rem(me + k, groups)
        return remote(
            out_rows.at[owner], in_rows.at[me], a_send.at[k], a_recv.at[k], {"emb": owner}
        )

    def a_start(k, carry):
        a_copy(lax.rem(k + 14, groups - 1) + 1).start()
        return carry

    lax.fori_loop(1, groups, a_start, 0)
    in_rows[me] = out_rows[me]
    lax.fori_loop(first_advance(chunks + lead_end), advances, advance, 0)

    def a_wait(k, carry):
        a_copy(k).wait_recv()
        return carry

    lax.fori_loop(1, groups, a_wait, 0)

    tower_out = pltpu.make_async_copy(t_final, tower_ref, out_sem)
    tower_out.start()

    hop = turns // 2
    reach = turns - hop
    cut = shard // 16 * 8
    order = sorted(range(nz), key=lambda k: (-min(k, nz - k), k))
    near = order[2 * reach - 1 :]
    wide = halves(in_rows[...].reshape(slots, 128))

    def s_copy(n, k):
        return remote(
            sums.at[n, pl.ds(0, shard)], swap.at[k], s_send.at[k], s_recv.at[k], partner
        )

    def q_copy(side, j):
        k = hop + j if side == 0 else nz - hop - j
        if j == reach:
            rows = pl.ds(0, cut) if side == 0 else pl.ds(cut, shard - cut)
            src, dst = mixed.at[k, rows], merge.at[side, j, rows]
        else:
            src, dst = mixed.at[k], merge.at[side, j]
        return remote(
            src, dst, q_send.at[side, j], q_recv.at[side, j], peer(j if side == 0 else nz - j)
        )

    def z_copy(k):
        return remote(mixed.at[k], from_z.at[k], z_send.at[k], z_recv.at[k], peer(k))

    def g_copy(k):
        place = final.at[replica]
        return remote(place, place, g_send.at[k], g_recv.at[k], peer(k))

    def e_copy(side, j):
        place = final.at[away(nz - hop if side == 0 else hop) * 2 + at_low]
        if j == reach:
            place = place.at[pl.ds(0, cut) if side == 0 else pl.ds(cut, shard - cut)]
        return remote(
            place, place, e_send.at[side, j], e_recv.at[side, j], peer(j if side == 0 else nz - j)
        )

    def f_copy(k):
        place = final.at[away(nz - k) * 2 + at_low]
        return remote(place, place, f_send.at[k], f_recv.at[k], partner)

    parts = 3 if nz % 3 == 0 else 2
    size = nz // parts
    for n in range(parts):
        both = jnp.dot(
            landing[n * size : (n + 1) * size].reshape(size * 2 * shard, slots),
            wide,
            preferred_element_type=F32,
        )
        sums[n * size : (n + 1) * size] = (both[:, :128] + both[:, 128:]).reshape(
            size, 2 * shard, 128
        )
        for m in range(n * size, (n + 1) * size):
            s_copy(m, order[m]).start()

    for n, k in enumerate(order):
        s_copy(n, k).wait_recv()
        mixed[k] = sums[n, pl.ds(shard, shard), :] + swap[k]
        if k == turns:
            q_copy(0, reach).start()
            q_copy(1, reach).start()
        elif hop < k < turns:
            q_copy(0, k - hop).start()
        elif turns < k < nz - hop:
            q_copy(1, nz - hop - k).start()
        elif k not in (0, hop, nz - hop):
            z_copy(k).start()
        if n == max(2 * reach, nz - 4):
            for side in range(2):
                mid = (hop, nz - hop)[side]
                for j in range(reach, 0, -1):
                    q_copy(side, j).wait_recv()
                    if j == reach:
                        rows = pl.ds(0, cut) if side == 0 else pl.ds(cut, shard - cut)
                        mixed[mid, rows] = mixed[mid, rows] + merge[side, j, rows]
                    else:
                        mixed[mid] = mixed[mid] + merge[side, j]
                z_copy(mid).start()
    total = mixed[0]
    for k in near[::-1]:
        if k:
            z_copy(k).wait_recv()
            total = total + from_z[k]
    final[replica] = total
    for k in near:
        if k:
            g_copy(k).start()
    f_copy(0).start()
    for side in range(2):
        mid = (hop, nz - hop)[side]
        g_copy(mid).wait_recv()
        for j in range(reach, 0, -1):
            e_copy(side, j).start()
        f_copy(mid).start()

    def drain(j, carry):
        w_copy(j).wait_send()
        for kind in range(4):
            x_copy(j, kind).wait_send()
        for kind in range(3):
            y_copy(j, kind).wait_send()
        return carry

    def a_drain(k, carry):
        a_copy(k).wait_send()
        return carry

    def t_drain(h, carry):
        for way in range(2):
            r_first(h, way).wait_send()
            h_last(h, way).wait_send()
            h_copy(0, h, way).wait_send()
        b_copy(h).wait_send()

        def inner(s, carry):
            for way in range(2):
                r_copy(s, h, way).wait_send()
            return carry

        def inner_h(s, carry):
            for way in range(2):
                h_copy(s, h, way).wait_send()
            return carry

        lax.fori_loop(1, turns, inner, 0)
        lax.fori_loop(1, turns - 1, inner_h, 0)
        return carry

    pair_copy().wait_send()
    lax.fori_loop(0, chunks, drain, 0)
    lax.fori_loop(1, groups, a_drain, 0)
    lax.fori_loop(0, 2, t_drain, 0)
    for k in near[::-1]:
        if k not in (0, hop, nz - hop):
            g_copy(k).wait_recv()
            f_copy(k).start()
    for j in range(1, reach):
        for side in range(2):
            e_copy(side, j).wait_recv()
            f_copy(hop + j if side == 0 else nz - hop - j).start()
    e_copy(0, reach).wait_recv()
    e_copy(1, reach).wait_recv()
    f_copy(turns).start()
    for k in order[::-1]:
        f_copy(k).wait_recv()
    for n, k in enumerate(order):
        s_copy(n, k).wait_send()
        f_copy(k).wait_send()
        if k and k in near:
            z_copy(k).wait_send()
            g_copy(k).wait_send()
    for side in range(2):
        for j in range(1, reach + 1):
            q_copy(side, j).wait_send()
            e_copy(side, j).wait_send()
    tower_out.wait()
    total_ref[...] = final[...]


def finish_kernel(total_ref, tower_ref, table_ref, accum_ref, weight_ref, new_table_ref, new_accum_ref, sem):
    out = pltpu.make_async_copy(tower_ref.at[pl.ds(0, weight_ref.shape[0])], weight_ref, sem)
    out.start()
    diagonal = lax.broadcasted_iota(jnp.int32, (128, 128), 0) == lax.broadcasted_iota(
        jnp.int32, (128, 128), 1
    )
    ones = jnp.ones((128, 128), F32)
    for n in range(accum_ref.shape[0]):
        rows = pl.ds(n * 128, 128)
        row_grad = total_ref[rows, :]
        terms = row_grad * row_grad * (1.0 / 128.0) + jnp.where(
            diagonal, jnp.broadcast_to(accum_ref[n : n + 1, :], (128, 128)), 0.0
        )
        grown = jnp.dot(terms, ones, precision=lax.Precision.HIGHEST, preferred_element_type=F32)
        new_table_ref[rows, :] = table_ref[rows, :] - learn_rate * row_grad / jnp.sqrt(grown)
        new_accum_ref[n : n + 1, :] = jnp.sum(
            jnp.where(diagonal, grown, 0.0), axis=0, keepdims=True
        )
    out.wait()


def finish(total, tower, table, accum, columns):
    vmem = pltpu.VMEM
    return pl.pallas_call(
        finish_kernel,
        out_shape=(
            jax.ShapeDtypeStruct((columns, 128), F32),
            jax.ShapeDtypeStruct(table.shape, F32),
            jax.ShapeDtypeStruct(accum.shape, F32),
        ),
        in_specs=[
            pl.BlockSpec(memory_space=vmem),
            pl.BlockSpec(memory_space=pl.ANY),
            pl.BlockSpec(memory_space=vmem),
            pl.BlockSpec(memory_space=vmem),
        ],
        out_specs=[
            pl.BlockSpec(memory_space=pl.ANY),
            pl.BlockSpec(memory_space=vmem),
            pl.BlockSpec(memory_space=vmem),
        ],
        scratch_shapes=[pltpu.SemaphoreType.DMA],
        compiler_params=pltpu.CompilerParams(vmem_limit_bytes=32 << 20),
    )(total, tower, table, accum)


def step(pooled, upstream, preact, tower_w, block_ids, ids, local_rows, dense, ny, nx):
    samples = upstream.shape[0]
    groups = ny * nx * 2
    nz = dense // 2
    batch = samples // groups
    columns = tower_w.shape[0]
    chunks = columns // CHUNK
    entries = block_ids.shape[1]
    slots = groups * CAP
    shard = -(-local_rows // (dense * 8)) * 8
    piece = -(-(columns + 8) // (nz * 32)) * 16
    turns = nz // 2
    vmem = pltpu.VMEM
    dma = pltpu.SemaphoreType.DMA
    total, tower = pl.pallas_call(
        functools.partial(step_kernel, ny, nx, nz, local_rows),
        out_shape=(
            jax.ShapeDtypeStruct((dense, shard, 128), F32),
            jax.ShapeDtypeStruct((nz * 2 * piece, 128), F32),
        ),
        in_specs=[pl.BlockSpec(memory_space=pl.ANY)] + [pl.BlockSpec(memory_space=vmem)] * 5,
        out_specs=[pl.BlockSpec(memory_space=vmem), pl.BlockSpec(memory_space=pl.ANY)],
        scratch_shapes=[
            vmem(pooled.shape, BF16),
            vmem((groups, batch, 128), F32),
            vmem((nx * ny, batch, 128), F32),
            vmem((nx * ny, batch, 128), F32),
            vmem((chunks, CHUNK, 128), F32),
            vmem((chunks, CHUNK, 128), F32),
            vmem((nx * ny * batch, 128), F32),
            vmem((chunks, CHUNK, 256), BF16),
            vmem((chunks, nx, ny * batch, CHUNK), F32),
            vmem((chunks, 2, 2 * batch, CHUNK), F32),
            vmem((chunks, 2, ny * batch, CHUNK), F32),
            vmem((chunks, 3, batch, CHUNK), F32),
            vmem((columns // 128, batch, 128), F32),
            vmem((slots, entries), BF16),
            vmem((groups, CAP, 128), F32),
            vmem((groups, CAP, 128), F32),
            vmem((8, slots), jnp.int32),
            vmem((nz, 2 * shard, slots), BF16),
            vmem((nz, 2 * shard, 128), F32),
            vmem((nz, shard, 128), F32),
            vmem((nz, shard, 128), F32),
            vmem((nz, shard, 128), F32),
            vmem((2, turns - turns // 2 + 1, shard, 128), F32),
            vmem((dense, shard, 128), F32),
            vmem((nz * 2 * piece, 128), F32),
            vmem((2, turns, 2, piece, 128), F32),
            vmem((2, piece, 128), F32),
            vmem((nz * 2 * piece, 128), F32),
            dma,
            dma,
            dma((chunks,)),
            dma((chunks,)),
            dma((4, chunks)),
            dma((4, chunks)),
            dma((3, chunks)),
            dma((3, chunks)),
            dma((groups,)),
            dma((groups,)),
        ]
        + [dma((nz,))] * 8
        + [
            dma((2, turns, 2)),
            dma((2, turns, 2)),
            dma((2,)),
            dma((2,)),
            dma((2, turns, 2)),
            dma((2, turns, 2)),
        ]
        + [dma((2, turns - turns // 2 + 1))] * 4
        + [dma, dma],
        compiler_params=pltpu.CompilerParams(
            collective_id=0, has_side_effects=True, vmem_limit_bytes=58 << 20
        ),
        cost_estimate=pl.CostEstimate(flops=1 << 30, bytes_accessed=8 << 20, transcendentals=0),
    )(pooled, upstream, preact, tower_w, block_ids, ids)
    return total.reshape(dense * shard, 128), tower


def shards(pooled, upstream, preact, tower_w, row_ids, table, accum):
    groups = lax.axis_size("emb")
    dense = lax.axis_size("dense")
    local_rows = table.shape[0]
    ids = row_ids.reshape(groups, -1, row_ids.shape[1]).transpose(0, 2, 1).reshape(groups, -1)
    block_ids = lax.dynamic_slice_in_dim(ids, lax.axis_index("emb"), 1, 0)
    total, tower = step(
        pooled, upstream, preact, tower_w, block_ids, ids, local_rows, dense, 4, 4
    )
    columns = tower_w.shape[0]
    weight_grad, new_table, new_accum = finish(
        total, tower, table, accum.reshape(-1, 128), columns
    )
    return (weight_grad, tower[columns], new_table, new_accum.reshape(-1))


def solution(mesh):
    placed = (
        P("dense", None),
        P("dense", "emb"),
        P("dense", "emb"),
        P(None, "emb"),
        P("dense", None),
        P("emb", None),
        P("emb"),
    )
    return jax.shard_map(
        shards,
        mesh=mesh,
        in_specs=placed,
        out_specs=(P(None, "emb"), P("emb"), P("emb", None), P("emb")),
        check_vma=False,
    )
```

```python
import functools

import jax
import jax.numpy as jnp
from jax import lax
from jax.experimental import pallas as pl
from jax.experimental.pallas import tpu as pltpu
from jax.sharding import PartitionSpec as P

learn_rate = 0.5
MESH = pl.DeviceIdType.MESH
CHUNK = 256
CAP = 40
F32 = jnp.float32
BF16 = jnp.bfloat16


def silu_slope(preact_f):
    sigmoid_val = jax.nn.sigmoid(preact_f)
    return sigmoid_val * (1.0 + preact_f * (1.0 - sigmoid_val))


def remote(src, dst, send, recv, where):
    return pltpu.make_async_remote_copy(
        src_ref=src, dst_ref=dst, send_sem=send, recv_sem=recv, device_id=where, device_id_type=MESH
    )


def place_rows(ids, groups, local_rows):
    entries = ids.shape[1]
    owners = ids // local_rows
    member = (lax.broadcasted_iota(jnp.int32, (groups, entries), 0) == owners).astype(F32)
    earlier = (
        lax.broadcasted_iota(jnp.int32, (entries, entries), 0)
        < lax.broadcasted_iota(jnp.int32, (entries, entries), 1)
    ).astype(F32).astype(BF16)
    prior = jnp.dot(member.astype(BF16), earlier, preferred_element_type=F32)
    ranks = jnp.sum(prior * member, axis=0, keepdims=True).astype(jnp.int32)
    slot_of = owners * CAP + ranks
    return (
        (lax.broadcasted_iota(jnp.int32, (groups * CAP, entries), 0) == slot_of)
        .astype(F32)
        .astype(BF16)
    )


def halves(rows):
    high = rows.astype(BF16)
    low = (rows - high.astype(F32)).astype(BF16)
    return jnp.concatenate([high, low], axis=1)


def landing_rows(ids, mine, local_rows):
    blocks, entries = ids.shape
    owners = ids // local_rows
    member = (owners == mine).astype(F32)
    earlier = (
        lax.broadcasted_iota(jnp.int32, (entries, entries), 0)
        < lax.broadcasted_iota(jnp.int32, (entries, entries), 1)
    ).astype(F32).astype(BF16)
    prior = jnp.dot(member.astype(BF16), earlier, preferred_element_type=F32)
    ranks = jnp.where(member > 0.5, prior.astype(jnp.int32), -1)
    offsets = (ids - owners * local_rows + 1).astype(F32)
    slots = lax.broadcasted_iota(jnp.int32, (CAP, entries), 0)
    columns = []
    for block in range(blocks):
        hit = jnp.where(slots == ranks[block : block + 1], offsets[block : block + 1], 0.0)
        columns.append(jnp.sum(hit, axis=1, keepdims=True))
    return jnp.concatenate(columns, axis=0) - 1.0


def step_kernel(
    ny,
    nx,
    nz,
    local_rows,
    pooled_ref,
    upstream_ref,
    preact_ref,
    w_ref,
    ids_ref,
    total_ref,
    tower_ref,
    pooled,
    spread,
    give,
    take,
    w_give,
    w_take,
    left,
    lhs,
    right,
    part,
    relay,
    from_x,
    from_y,
    grads,
    placing,
    out_rows,
    in_rows,
    target,
    landing,
    sums,
    swap,
    mixed,
    from_z,
    merge,
    final,
    tower,
    t_from,
    t_swap,
    t_final,
    pair_send,
    pair_recv,
    w_send,
    w_recv,
    x_send,
    x_recv,
    y_send,
    y_recv,
    a_send,
    a_recv,
    s_send,
    s_recv,
    z_send,
    z_recv,
    g_send,
    g_recv,
    f_send,
    f_recv,
    r_send,
    r_recv,
    b_send,
    b_recv,
    h_send,
    h_recv,
    q_send,
    q_recv,
    e_send,
    e_recv,
    in_sem,
    out_sem,
):
    chunks = part.shape[0]
    groups = ny * nx * 2
    batch = upstream_ref.shape[0] // groups
    columns = w_ref.shape[0]
    me = lax.axis_index("emb")
    core = lax.rem(me, 2)
    at_x = lax.rem(me // 2, nx)
    at_y = me // (2 * nx)
    replica = lax.axis_index("dense")
    at_low = lax.rem(replica, 2)
    at_z = replica // 2

    def there(y, x, c):
        return {"emb": (lax.rem(y, ny) * nx + lax.rem(x, nx)) * 2 + c}

    sibling = there(at_y, at_x, 1 - core)

    ahead = 4

    def y_first(j):
        return lax.rem(j, 2) * ((chunks + ahead - 1 - j) // chunks)

    def along(turned, k):
        return there(at_y + turned * k, at_x + (1 - turned) * k, core)

    partner = {"dense": at_z * 2 + 1 - at_low}

    def away(k):
        return lax.rem(at_z + k, nz)

    def peer(k):
        return {"dense": away(k) * 2 + at_low}

    z_ends = (peer(1), peer(nz - 1))

    load = pltpu.make_async_copy(pooled_ref, pooled, in_sem)
    load.start()
    barrier = pltpu.get_barrier_semaphore()

    def greet(k, carry):
        pl.semaphore_signal(
            barrier, inc=1, device_id={"emb": lax.rem(me + k, groups)}, device_id_type=MESH
        )
        return carry

    def greet_z(k, carry):
        pl.semaphore_signal(barrier, inc=1, device_id=peer(k), device_id_type=MESH)
        return carry

    lax.fori_loop(1, groups, greet, 0)
    lax.fori_loop(1, nz, greet_z, 0)
    pl.semaphore_signal(barrier, inc=1, device_id=partner, device_id_type=MESH)

    slope = silu_slope(preact_ref[...].astype(F32))
    deltas = (upstream_ref[...].astype(F32) * slope).astype(BF16).astype(F32)
    spread[...] = deltas.reshape(groups, batch, 128)
    for q in range(nx):
        for p in range(ny):
            block = (lax.rem(at_y + p, ny) * nx + lax.rem(at_x + q, nx)) * 2
            give[q * ny + p] = spread[block + 1 - core]
            left[pl.ds((q * ny + p) * batch, batch), :] = spread[block + core]
    w_give[...] = w_ref[...].astype(F32).reshape(w_give.shape)
    right[:, :, :128] = w_ref[...].reshape(chunks, CHUNK, 128)

    pl.semaphore_wait(barrier, groups - 1 + nz)

    turns = nz // 2
    part_rows = t_swap.shape[1]
    bit = part_rows // 2

    def stretch(t, h, first=0, size=part_rows):
        return pl.ds(pl.multiple_of((t * 2 + h) * part_rows + first, 8), size)

    def ring_at(way, k):
        return away(k) if way == 0 else away(nz - k)

    def r_copy(s, h, way):
        return remote(
            tower.at[stretch(ring_at(way, turns - s), h)],
            t_from.at[way, s, h],
            r_send.at[way, s, h],
            r_recv.at[way, s, h],
            z_ends[way],
        )

    def r_first(h, way):
        rows = pl.ds(way * bit, bit)
        return remote(
            tower.at[stretch(away(turns), h, way * bit, bit)],
            t_from.at[way, 0, h, rows],
            r_send.at[way, 0, h],
            r_recv.at[way, 0, h],
            z_ends[way],
        )

    def b_copy(h):
        place = tower.at[stretch(at_z, h)]
        return remote(place, t_swap.at[h], b_send.at[h], b_recv.at[h], partner)

    def h_copy(s, h, way):
        place = t_final.at[stretch(ring_at(1 - way, s), h)]
        return remote(place, place, h_send.at[way, s, h], h_recv.at[way, s, h], z_ends[way])

    def h_last(h, way):
        place = t_final.at[stretch(ring_at(1 - way, turns - 1), h, way * bit, bit)]
        return remote(
            place,
            place,
            h_send.at[way, turns - 1, h],
            h_recv.at[way, turns - 1, h],
            z_ends[way],
        )

    def advance(n, carry):
        h = lax.rem(n, 2)
        s = n // 2

        @pl.when(s == 0)
        def _():
            for way in range(2):
                r_first(h, way).start()

        @pl.when(s == 1)
        def _():
            for way in range(2):
                r_first(h, way).wait_recv()
                t = ring_at(way, turns - 1)
                rows = pl.ds(way * bit, bit)
                here = stretch(t, h, way * bit, bit)
                tower[here, :] = tower[here, :] + t_from[way, 0, h, rows]
                r_copy(1, h, way).start()

        @pl.when(jnp.logical_and(s >= 2, s < turns))
        def _():
            for way in range(2):
                r_copy(s - 1, h, way).wait_recv()
                t = ring_at(way, turns - s)
                tower[stretch(t, h), :] = tower[stretch(t, h), :] + t_from[way, s - 1, h]
                r_copy(s, h, way).start()

        @pl.when(s == turns)
        def _():
            r_copy(turns - 1, h, 0).wait_recv()
            r_copy(turns - 1, h, 1).wait_recv()
            here = stretch(at_z, h)
            tower[here, :] = (
                tower[here, :] + t_from[0, turns - 1, h] + t_from[1, turns - 1, h]
            )
            b_copy(h).start()

        @pl.when(s == turns + 1)
        def _():
            b_copy(h).wait_recv()
            t_final[stretch(at_z, h), :] = tower[stretch(at_z, h), :] + t_swap[h]
            for way in range(2):
                h_copy(0, h, way).start()

        @pl.when(jnp.logical_and(s >= turns + 2, s < 2 * turns))
        def _():
            for way in range(2):
                h_copy(s - turns - 2, h, way).wait_recv()
                h_copy(s - turns - 1, h, way).start()

        @pl.when(s == 2 * turns)
        def _():
            for way in range(2):
                h_copy(turns - 2, h, way).wait_recv()
                h_last(h, way).start()

        @pl.when(s == 2 * turns + 1)
        def _():
            for way in range(2):
                h_last(h, way).wait_recv()

        return carry

    advances = 2 * (2 * turns + 2)

    def pair_copy():
        return remote(give, take, pair_send, pair_recv, sibling)

    def w_copy(j):
        return remote(w_give.at[j], w_take.at[j], w_send.at[j], w_recv.at[j], sibling)

    half = 2 * batch

    def x_copy(j, kind):
        if kind == 0:
            src, dst = part.at[j, 2, pl.ds(0, half)], relay.at[j, 0]
        elif kind == 1:
            src, dst = part.at[j, 2, pl.ds(half, half)], relay.at[j, 1]
        elif kind == 2:
            src, dst = part.at[j, 1], from_x.at[j, 0]
        else:
            src, dst = part.at[j, 3], from_x.at[j, 1]
        where = along(y_first(j), 3 if kind % 2 else 1)
        return remote(src, dst, x_send.at[kind, j], x_recv.at[kind, j], where)

    def y_copy(j, kind):
        where = along(1 - y_first(j), kind + 1)
        src = part.at[j, 0, pl.ds((kind + 1) * batch, batch)]
        return remote(src, from_y.at[j, kind], y_send.at[kind, j], y_recv.at[kind, j], where)

    pair_copy().start()

    def w_start(j, carry):
        w_copy(j).start()
        return carry

    lax.fori_loop(0, chunks, w_start, 0)
    pair_copy().wait_recv()
    for n in range(2):
        blocks = [q * ny + p for q in range(nx) for p in range(ny)]
        if n:
            blocks = [q * ny + p for p in range(ny) for q in range(nx)]
        own = jnp.concatenate([left[k * batch : (k + 1) * batch] for k in blocks], axis=0)
        pair = jnp.concatenate([take[k] for k in blocks], axis=0)
        lhs[n, :, :128] = own.astype(BF16)
        lhs[n, :, 128:] = pair.astype(BF16)
    lead_s2, lead_y, lead_end = ahead, ahead + 3, ahead + 6
    slots = groups * CAP
    shard = swap.shape[1]

    def first_advance(i):
        return jnp.minimum(2 + (3 * (i - ahead)) // 2, advances)

    def multiply(i, carry):
        w_copy(i).wait_recv()
        right[i, :, 128:] = w_take[i].astype(BF16)
        product = lax.dot_general(
            lhs[y_first(i)],
            right[i],
            (((1,), (1,)), ((), ())),
            preferred_element_type=F32,
        )
        part[i] = product.reshape(part.shape[1:])
        x_copy(i, 0).start()
        x_copy(i, 1).start()
        return carry

    lax.fori_loop(0, ahead, multiply, 0)

    spare = tower.shape[0] - columns
    every = spread[...].reshape(groups * batch, 128)
    tower[pl.ds(columns, spare), :] = jnp.where(
        lax.broadcasted_iota(jnp.int32, (spare, 128), 0) == 0,
        jnp.broadcast_to(jnp.sum(every, axis=0, keepdims=True), (spare, 128)),
        0.0,
    )
    turned = every.T.astype(BF16)
    load.wait()
    for j in range(chunks):
        flat = jnp.dot(
            turned, pooled[:, j * CHUNK : (j + 1) * CHUNK], preferred_element_type=F32
        )
        tower[j * CHUNK : (j + 1) * CHUNK, :] = flat.T
    lax.fori_loop(0, 2, advance, 0)

    def step(i, carry):
        @pl.when(i < chunks)
        def _():
            multiply(i, 0)

        @pl.when(jnp.logical_and(i >= lead_s2, i < chunks + lead_s2))
        def _():
            j = i - lead_s2
            x_copy(j, 0).wait_recv()
            part[j, 1, pl.ds(0, half)] = part[j, 1, pl.ds(0, half)] + relay[j, 0]
            x_copy(j, 2).start()
            x_copy(j, 1).wait_recv()
            part[j, 3, pl.ds(half, half)] = part[j, 3, pl.ds(half, half)] + relay[j, 1]
            x_copy(j, 3).start()

        lax.fori_loop(first_advance(i), first_advance(i + 1), advance, 0)

        @pl.when(i == 5)
        def _():
            placing[...] = place_rows(ids_ref[pl.ds(me, 1), :], groups, local_rows)

        @pl.when(i == 6)
        def _():
            wide = jnp.broadcast_to(landing_rows(ids_ref[...], me, local_rows), (slots, 128))
            target[...] = wide.T[0:8].astype(jnp.int32)

        @pl.when(jnp.logical_and(i >= 7, i < 7 + nz))
        def _():
            n = i - 7
            k = turns + jnp.where(lax.rem(n, 2) == 0, (n + 1) // 2, -((n + 1) // 2))
            rows = lax.broadcasted_iota(jnp.int32, (shard, slots), 0)
            for low in range(2):
                owned = 1 - at_low if low == 0 else at_low
                hit = rows + (away(k) * 2 + owned) * shard == target[0:1]
                landing[n, pl.ds(low * shard, shard), :] = hit.astype(F32).astype(BF16)

        @pl.when(jnp.logical_and(i >= lead_y, i < chunks + lead_y))
        def _():
            j = i - lead_y
            x_copy(j, 2).wait_recv()
            x_copy(j, 3).wait_recv()
            part[j, 0] = part[j, 0] + from_x[j, 0] + from_x[j, 1]
            for kind in (1, 0, 2):
                y_copy(j, kind).start()

        @pl.when(i >= lead_end)
        def _():
            j = i - lead_end
            for kind in range(3):
                y_copy(j, kind).wait_recv()
            total = part[j, 0, pl.ds(0, batch)] + from_y[j, 0] + from_y[j, 1] + from_y[j, 2]
            for n in range(CHUNK // 128):
                grads[j * (CHUNK // 128) + n] = total[:, n * 128 : (n + 1) * 128]

        return carry

    lax.fori_loop(ahead, chunks + lead_end, step, 0)

    wide = halves(grads[...].reshape(-1, 128))
    both = jnp.dot(placing[...], wide, preferred_element_type=F32)
    out_rows[...] = (both[:, :128] + both[:, 128:]).reshape(out_rows.shape)

    def a_copy(k):
        owner = lax.rem(me + k, groups)
        return remote(
            out_rows.at[owner], in_rows.at[me], a_send.at[k], a_recv.at[k], {"emb": owner}
        )

    def a_start(k, carry):
        a_copy(lax.rem(k + 14, groups - 1) + 1).start()
        return carry

    lax.fori_loop(1, groups, a_start, 0)
    in_rows[me] = out_rows[me]
    lax.fori_loop(first_advance(chunks + lead_end), advances, advance, 0)

    def a_wait(k, carry):
        a_copy(k).wait_recv()
        return carry

    lax.fori_loop(1, groups, a_wait, 0)

    tower_out = pltpu.make_async_copy(t_final, tower_ref, out_sem)
    tower_out.start()

    hop = turns // 2
    reach = turns - hop
    cut = shard // 16 * 8
    order = sorted(range(nz), key=lambda k: (-min(k, nz - k), k))
    near = order[2 * reach - 1 :]
    wide = halves(in_rows[...].reshape(slots, 128))

    def s_copy(n, k):
        return remote(
            sums.at[n, pl.ds(0, shard)], swap.at[k], s_send.at[k], s_recv.at[k], partner
        )

    def q_copy(side, j):
        k = hop + j if side == 0 else nz - hop - j
        if j == reach:
            rows = pl.ds(0, cut) if side == 0 else pl.ds(cut, shard - cut)
            src, dst = mixed.at[k, rows], merge.at[side, j, rows]
        else:
            src, dst = mixed.at[k], merge.at[side, j]
        return remote(
            src, dst, q_send.at[side, j], q_recv.at[side, j], peer(j if side == 0 else nz - j)
        )

    def z_copy(k):
        return remote(mixed.at[k], from_z.at[k], z_send.at[k], z_recv.at[k], peer(k))

    def g_copy(k):
        place = final.at[replica]
        return remote(place, place, g_send.at[k], g_recv.at[k], peer(k))

    def e_copy(side, j):
        place = final.at[away(nz - hop if side == 0 else hop) * 2 + at_low]
        if j == reach:
            place = place.at[pl.ds(0, cut) if side == 0 else pl.ds(cut, shard - cut)]
        return remote(
            place, place, e_send.at[side, j], e_recv.at[side, j], peer(j if side == 0 else nz - j)
        )

    def f_copy(k):
        place = final.at[away(nz - k) * 2 + at_low]
        return remote(place, place, f_send.at[k], f_recv.at[k], partner)

    parts = 3 if nz % 3 == 0 else 2
    size = nz // parts
    for n in range(parts):
        both = jnp.dot(
            landing[n * size : (n + 1) * size].reshape(size * 2 * shard, slots),
            wide,
            preferred_element_type=F32,
        )
        sums[n * size : (n + 1) * size] = (both[:, :128] + both[:, 128:]).reshape(
            size, 2 * shard, 128
        )
        for m in range(n * size, (n + 1) * size):
            s_copy(m, order[m]).start()

    for n, k in enumerate(order):
        s_copy(n, k).wait_recv()
        mixed[k] = sums[n, pl.ds(shard, shard), :] + swap[k]
        if k == turns:
            q_copy(0, reach).start()
            q_copy(1, reach).start()
        elif hop < k < turns:
            q_copy(0, k - hop).start()
        elif turns < k < nz - hop:
            q_copy(1, nz - hop - k).start()
        elif k not in (0, hop, nz - hop):
            z_copy(k).start()
        if n == max(2 * reach, nz - 4):
            for side in range(2):
                mid = (hop, nz - hop)[side]
                for j in range(reach, 0, -1):
                    q_copy(side, j).wait_recv()
                    if j == reach:
                        rows = pl.ds(0, cut) if side == 0 else pl.ds(cut, shard - cut)
                        mixed[mid, rows] = mixed[mid, rows] + merge[side, j, rows]
                    else:
                        mixed[mid] = mixed[mid] + merge[side, j]
                z_copy(mid).start()
    total = mixed[0]
    for k in near[::-1]:
        if k:
            z_copy(k).wait_recv()
            total = total + from_z[k]
    final[replica] = total
    for k in near:
        if k:
            g_copy(k).start()
    f_copy(0).start()
    for side in range(2):
        mid = (hop, nz - hop)[side]
        g_copy(mid).wait_recv()
        for j in range(reach, 0, -1):
            e_copy(side, j).start()
        f_copy(mid).start()

    def drain(j, carry):
        w_copy(j).wait_send()
        for kind in range(4):
            x_copy(j, kind).wait_send()
        for kind in range(3):
            y_copy(j, kind).wait_send()
        return carry

    def a_drain(k, carry):
        a_copy(k).wait_send()
        return carry

    def t_drain(h, carry):
        for way in range(2):
            r_first(h, way).wait_send()
            h_last(h, way).wait_send()
            h_copy(0, h, way).wait_send()
        b_copy(h).wait_send()

        def inner(s, carry):
            for way in range(2):
                r_copy(s, h, way).wait_send()
            return carry

        def inner_h(s, carry):
            for way in range(2):
                h_copy(s, h, way).wait_send()
            return carry

        lax.fori_loop(1, turns, inner, 0)
        lax.fori_loop(1, turns - 1, inner_h, 0)
        return carry

    pair_copy().wait_send()
    lax.fori_loop(0, chunks, drain, 0)
    lax.fori_loop(1, groups, a_drain, 0)
    lax.fori_loop(0, 2, t_drain, 0)
    for k in near[::-1]:
        if k not in (0, hop, nz - hop):
            g_copy(k).wait_recv()
            f_copy(k).start()
    for j in range(1, reach):
        for side in range(2):
            e_copy(side, j).wait_recv()
            f_copy(hop + j if side == 0 else nz - hop - j).start()
    e_copy(0, reach).wait_recv()
    e_copy(1, reach).wait_recv()
    f_copy(turns).start()
    for k in order[::-1]:
        f_copy(k).wait_recv()
    for n, k in enumerate(order):
        s_copy(n, k).wait_send()
        f_copy(k).wait_send()
        if k and k in near:
            z_copy(k).wait_send()
            g_copy(k).wait_send()
    for side in range(2):
        for j in range(1, reach + 1):
            q_copy(side, j).wait_send()
            e_copy(side, j).wait_send()
    tower_out.wait()
    total_ref[...] = final[...]


def finish_kernel(
    total_hbm,
    tower_hbm,
    table_hbm,
    accum_ref,
    weight_ref,
    new_table_ref,
    new_accum_ref,
    bias_ref,
    total_ref,
    table_ref,
    tower_ref,
    sems,
):
    columns = weight_ref.shape[0]
    local_rows = table_ref.shape[0]
    out = pltpu.make_async_copy(tower_ref.at[pl.ds(0, columns)], weight_ref, sems.at[0])
    loads = [
        pltpu.make_async_copy(tower_hbm.at[pl.ds(0, columns + 8)], tower_ref, sems.at[3]),
        pltpu.make_async_copy(total_hbm.at[pl.ds(0, local_rows)], total_ref, sems.at[1]),
        pltpu.make_async_copy(table_hbm, table_ref, sems.at[2]),
    ]
    for load in loads:
        load.start()
    diagonal = lax.broadcasted_iota(jnp.int32, (128, 128), 0) == lax.broadcasted_iota(
        jnp.int32, (128, 128), 1
    )
    ones = jnp.ones((128, 128), F32)
    for load in loads:
        load.wait()
    out.start()
    bias_ref[...] = tower_ref[pl.ds(columns, 1), :]
    for n in range(accum_ref.shape[0]):
        rows = pl.ds(n * 128, 128)
        row_grad = total_ref[rows, :]
        terms = row_grad * row_grad * (1.0 / 128.0) + jnp.where(
            diagonal, jnp.broadcast_to(accum_ref[n : n + 1, :], (128, 128)), 0.0
        )
        grown = jnp.dot(terms, ones, precision=lax.Precision.HIGHEST, preferred_element_type=F32)
        new_table_ref[rows, :] = table_ref[rows, :] - learn_rate * row_grad / jnp.sqrt(grown)
        new_accum_ref[n : n + 1, :] = jnp.sum(
            jnp.where(diagonal, grown, 0.0), axis=0, keepdims=True
        )
    out.wait()


def finish(total, tower, table, accum, columns):
    vmem = pltpu.VMEM
    return pl.pallas_call(
        finish_kernel,
        out_shape=(
            jax.ShapeDtypeStruct((columns, 128), F32),
            jax.ShapeDtypeStruct(table.shape, F32),
            jax.ShapeDtypeStruct(accum.shape, F32),
            jax.ShapeDtypeStruct((1, 128), F32),
        ),
        in_specs=[pl.BlockSpec(memory_space=pl.ANY)] * 3 + [pl.BlockSpec(memory_space=vmem)],
        out_specs=[pl.BlockSpec(memory_space=pl.ANY)] + [pl.BlockSpec(memory_space=vmem)] * 3,
        scratch_shapes=[
            vmem(table.shape, F32),
            vmem(table.shape, F32),
            vmem((columns + 8, 128), F32),
            pltpu.SemaphoreType.DMA((4,)),
        ],
        compiler_params=pltpu.CompilerParams(vmem_limit_bytes=58 << 20),
    )(total, tower, table, accum)


def step(pooled, upstream, preact, tower_w, ids, local_rows, dense, ny, nx):
    samples = upstream.shape[0]
    groups = ny * nx * 2
    nz = dense // 2
    batch = samples // groups
    columns = tower_w.shape[0]
    chunks = columns // CHUNK
    entries = ids.shape[1]
    slots = groups * CAP
    shard = -(-local_rows // (dense * 8)) * 8
    piece = -(-(columns + 8) // (nz * 32)) * 16
    turns = nz // 2
    vmem = pltpu.VMEM
    dma = pltpu.SemaphoreType.DMA
    total, tower = pl.pallas_call(
        functools.partial(step_kernel, ny, nx, nz, local_rows),
        out_shape=(
            jax.ShapeDtypeStruct((dense, shard, 128), F32),
            jax.ShapeDtypeStruct((nz * 2 * piece, 128), F32),
        ),
        in_specs=[pl.BlockSpec(memory_space=pl.ANY)] + [pl.BlockSpec(memory_space=vmem)] * 4,
        out_specs=[pl.BlockSpec(memory_space=vmem), pl.BlockSpec(memory_space=pl.ANY)],
        scratch_shapes=[
            vmem(pooled.shape, BF16),
            vmem((groups, batch, 128), F32),
            vmem((nx * ny, batch, 128), F32),
            vmem((nx * ny, batch, 128), F32),
            vmem((chunks, CHUNK, 128), F32),
            vmem((chunks, CHUNK, 128), F32),
            vmem((nx * ny * batch, 128), F32),
            vmem((2, nx * ny * batch, 256), BF16),
            vmem((chunks, CHUNK, 256), BF16),
            vmem((chunks, nx, ny * batch, CHUNK), F32),
            vmem((chunks, 2, 2 * batch, CHUNK), F32),
            vmem((chunks, 2, ny * batch, CHUNK), F32),
            vmem((chunks, 3, batch, CHUNK), F32),
            vmem((columns // 128, batch, 128), F32),
            vmem((slots, entries), BF16),
            vmem((groups, CAP, 128), F32),
            vmem((groups, CAP, 128), F32),
            vmem((8, slots), jnp.int32),
            vmem((nz, 2 * shard, slots), BF16),
            vmem((nz, 2 * shard, 128), F32),
            vmem((nz, shard, 128), F32),
            vmem((nz, shard, 128), F32),
            vmem((nz, shard, 128), F32),
            vmem((2, turns - turns // 2 + 1, shard, 128), F32),
            vmem((dense, shard, 128), F32),
            vmem((nz * 2 * piece, 128), F32),
            vmem((2, turns, 2, piece, 128), F32),
            vmem((2, piece, 128), F32),
            vmem((nz * 2 * piece, 128), F32),
            dma,
            dma,
            dma((chunks,)),
            dma((chunks,)),
            dma((4, chunks)),
            dma((4, chunks)),
            dma((3, chunks)),
            dma((3, chunks)),
            dma((groups,)),
            dma((groups,)),
        ]
        + [dma((nz,))] * 8
        + [
            dma((2, turns, 2)),
            dma((2, turns, 2)),
            dma((2,)),
            dma((2,)),
            dma((2, turns, 2)),
            dma((2, turns, 2)),
        ]
        + [dma((2, turns - turns // 2 + 1))] * 4
        + [dma, dma],
        compiler_params=pltpu.CompilerParams(
            collective_id=0, has_side_effects=True, vmem_limit_bytes=58 << 20
        ),
        cost_estimate=pl.CostEstimate(flops=1 << 30, bytes_accessed=8 << 20, transcendentals=0),
    )(pooled, upstream, preact, tower_w, ids)
    return total.reshape(dense * shard, 128), tower


def shards(pooled, upstream, preact, tower_w, row_ids, table, accum):
    groups = lax.axis_size("emb")
    dense = lax.axis_size("dense")
    local_rows = table.shape[0]
    ids = row_ids.reshape(groups, -1, row_ids.shape[1]).transpose(0, 2, 1).reshape(groups, -1)
    total, tower = step(
        pooled, upstream, preact, tower_w, ids, local_rows, dense, 4, 4
    )
    columns = tower_w.shape[0]
    weight_grad, new_table, new_accum, bias_grad = finish(
        total, tower, table, accum.reshape(-1, 128), columns
    )
    return (weight_grad, bias_grad.reshape(-1), new_table, new_accum.reshape(-1))


def solution(mesh):
    placed = (
        P("dense", None),
        P("dense", "emb"),
        P("dense", "emb"),
        P(None, "emb"),
        P("dense", None),
        P("emb", None),
        P("emb"),
    )
    return jax.shard_map(
        shards,
        mesh=mesh,
        in_specs=placed,
        out_specs=(P(None, "emb"), P("emb"), P("emb", None), P("emb")),
        check_vma=False,
    )
```

```python
import functools

import jax
import jax.numpy as jnp
from jax import lax
from jax.experimental import pallas as pl
from jax.experimental.pallas import tpu as pltpu
from jax.sharding import PartitionSpec as P

learn_rate = 0.5
MESH = pl.DeviceIdType.MESH
CHUNK = 256
CAP = 40
F32 = jnp.float32
BF16 = jnp.bfloat16


def silu_slope(preact_f):
    sigmoid_val = jax.nn.sigmoid(preact_f)
    return sigmoid_val * (1.0 + preact_f * (1.0 - sigmoid_val))


def remote(src, dst, send, recv, where):
    return pltpu.make_async_remote_copy(
        src_ref=src, dst_ref=dst, send_sem=send, recv_sem=recv, device_id=where, device_id_type=MESH
    )


def place_rows(ids, groups, local_rows):
    entries = ids.shape[1]
    owners = ids // local_rows
    member = (lax.broadcasted_iota(jnp.int32, (groups, entries), 0) == owners).astype(F32)
    earlier = (
        lax.broadcasted_iota(jnp.int32, (entries, entries), 0)
        < lax.broadcasted_iota(jnp.int32, (entries, entries), 1)
    ).astype(F32).astype(BF16)
    prior = jnp.dot(member.astype(BF16), earlier, preferred_element_type=F32)
    ranks = jnp.sum(prior * member, axis=0, keepdims=True).astype(jnp.int32)
    slot_of = owners * CAP + ranks
    return (
        (lax.broadcasted_iota(jnp.int32, (groups * CAP, entries), 0) == slot_of)
        .astype(F32)
        .astype(BF16)
    )


def halves(rows):
    high = rows.astype(BF16)
    low = (rows - high.astype(F32)).astype(BF16)
    return jnp.concatenate([high, low], axis=1)


def landing_rows(ids, mine, local_rows):
    blocks, entries = ids.shape
    owners = ids // local_rows
    member = (owners == mine).astype(F32)
    earlier = (
        lax.broadcasted_iota(jnp.int32, (entries, entries), 0)
        < lax.broadcasted_iota(jnp.int32, (entries, entries), 1)
    ).astype(F32).astype(BF16)
    prior = jnp.dot(member.astype(BF16), earlier, preferred_element_type=F32)
    ranks = jnp.where(member > 0.5, prior.astype(jnp.int32), -1)
    offsets = (ids - owners * local_rows + 1).astype(F32)
    slots = lax.broadcasted_iota(jnp.int32, (CAP, entries), 0)
    columns = []
    for block in range(blocks):
        hit = jnp.where(slots == ranks[block : block + 1], offsets[block : block + 1], 0.0)
        columns.append(jnp.sum(hit, axis=1, keepdims=True))
    return jnp.concatenate(columns, axis=0) - 1.0


def step_kernel(
    ny,
    nx,
    nz,
    local_rows,
    pooled_ref,
    upstream_ref,
    preact_ref,
    w_ref,
    ids_ref,
    total_ref,
    tower_ref,
    pooled,
    spread,
    give,
    take,
    w_give,
    w_take,
    left,
    lhs,
    right,
    part,
    relay,
    from_x,
    from_y,
    grads,
    placing,
    out_rows,
    in_rows,
    target,
    landing,
    sums,
    swap,
    mixed,
    from_z,
    merge,
    final,
    tower,
    t_from,
    t_swap,
    t_final,
    pair_send,
    pair_recv,
    w_send,
    w_recv,
    x_send,
    x_recv,
    y_send,
    y_recv,
    a_send,
    a_recv,
    s_send,
    s_recv,
    z_send,
    z_recv,
    g_send,
    g_recv,
    f_send,
    f_recv,
    r_send,
    r_recv,
    b_send,
    b_recv,
    h_send,
    h_recv,
    q_send,
    q_recv,
    e_send,
    e_recv,
    in_sem,
    out_sem,
):
    chunks = part.shape[0]
    groups = ny * nx * 2
    batch = upstream_ref.shape[0] // groups
    columns = w_ref.shape[0]
    me = lax.axis_index("emb")
    core = lax.rem(me, 2)
    at_x = lax.rem(me // 2, nx)
    at_y = me // (2 * nx)
    replica = lax.axis_index("dense")
    at_low = lax.rem(replica, 2)
    at_z = replica // 2

    def there(y, x, c):
        return {"emb": (lax.rem(y, ny) * nx + lax.rem(x, nx)) * 2 + c}

    sibling = there(at_y, at_x, 1 - core)

    ahead = 4

    def y_first(j):
        return lax.rem(j, 2) * ((chunks + ahead - 1 - j) // chunks)

    def along(turned, k):
        return there(at_y + turned * k, at_x + (1 - turned) * k, core)

    partner = {"dense": at_z * 2 + 1 - at_low}

    def away(k):
        return lax.rem(at_z + k, nz)

    def peer(k):
        return {"dense": away(k) * 2 + at_low}

    z_ends = (peer(1), peer(nz - 1))

    load = pltpu.make_async_copy(pooled_ref, pooled, in_sem)
    load.start()
    barrier = pltpu.get_barrier_semaphore()

    def greet(k, carry):
        pl.semaphore_signal(
            barrier, inc=1, device_id={"emb": lax.rem(me + k, groups)}, device_id_type=MESH
        )
        return carry

    def greet_z(k, carry):
        pl.semaphore_signal(barrier, inc=1, device_id=peer(k), device_id_type=MESH)
        return carry

    lax.fori_loop(1, groups, greet, 0)
    lax.fori_loop(1, nz, greet_z, 0)
    pl.semaphore_signal(barrier, inc=1, device_id=partner, device_id_type=MESH)

    slope = silu_slope(preact_ref[...].astype(F32))
    deltas = (upstream_ref[...].astype(F32) * slope).astype(BF16).astype(F32)
    spread[...] = deltas.reshape(groups, batch, 128)
    for q in range(nx):
        for p in range(ny):
            block = (lax.rem(at_y + p, ny) * nx + lax.rem(at_x + q, nx)) * 2
            give[q * ny + p] = spread[block + 1 - core]
            left[pl.ds((q * ny + p) * batch, batch), :] = spread[block + core]
    w_give[...] = w_ref[...].astype(F32).reshape(w_give.shape)
    right[:, :, :128] = w_ref[...].reshape(chunks, CHUNK, 128)

    pl.semaphore_wait(barrier, groups - 1 + nz)

    turns = nz // 2
    part_rows = t_swap.shape[1]
    bit = part_rows // 2

    def stretch(t, h, first=0, size=part_rows):
        return pl.ds(pl.multiple_of((t * 2 + h) * part_rows + first, 8), size)

    def ring_at(way, k):
        return away(k) if way == 0 else away(nz - k)

    def r_copy(s, h, way):
        return remote(
            tower.at[stretch(ring_at(way, turns - s), h)],
            t_from.at[way, s, h],
            r_send.at[way, s, h],
            r_recv.at[way, s, h],
            z_ends[way],
        )

    def r_first(h, way):
        rows = pl.ds(way * bit, bit)
        return remote(
            tower.at[stretch(away(turns), h, way * bit, bit)],
            t_from.at[way, 0, h, rows],
            r_send.at[way, 0, h],
            r_recv.at[way, 0, h],
            z_ends[way],
        )

    def b_copy(h):
        place = tower.at[stretch(at_z, h)]
        return remote(place, t_swap.at[h], b_send.at[h], b_recv.at[h], partner)

    def h_copy(s, h, way):
        place = t_final.at[stretch(ring_at(1 - way, s), h)]
        return remote(place, place, h_send.at[way, s, h], h_recv.at[way, s, h], z_ends[way])

    def h_last(h, way):
        place = t_final.at[stretch(ring_at(1 - way, turns - 1), h, way * bit, bit)]
        return remote(
            place,
            place,
            h_send.at[way, turns - 1, h],
            h_recv.at[way, turns - 1, h],
            z_ends[way],
        )

    def advance(n, carry):
        h = lax.rem(n, 2)
        s = n // 2

        @pl.when(s == 0)
        def _():
            for way in range(2):
                r_first(h, way).start()

        @pl.when(s == 1)
        def _():
            for way in range(2):
                r_first(h, way).wait_recv()
                t = ring_at(way, turns - 1)
                rows = pl.ds(way * bit, bit)
                here = stretch(t, h, way * bit, bit)
                tower[here, :] = tower[here, :] + t_from[way, 0, h, rows]
                r_copy(1, h, way).start()

        @pl.when(jnp.logical_and(s >= 2, s < turns))
        def _():
            for way in range(2):
                r_copy(s - 1, h, way).wait_recv()
                t = ring_at(way, turns - s)
                tower[stretch(t, h), :] = tower[stretch(t, h), :] + t_from[way, s - 1, h]
                r_copy(s, h, way).start()

        @pl.when(s == turns)
        def _():
            r_copy(turns - 1, h, 0).wait_recv()
            r_copy(turns - 1, h, 1).wait_recv()
            here = stretch(at_z, h)
            tower[here, :] = (
                tower[here, :] + t_from[0, turns - 1, h] + t_from[1, turns - 1, h]
            )
            b_copy(h).start()

        @pl.when(s == turns + 1)
        def _():
            b_copy(h).wait_recv()
            t_final[stretch(at_z, h), :] = tower[stretch(at_z, h), :] + t_swap[h]
            for way in range(2):
                h_copy(0, h, way).start()

        @pl.when(jnp.logical_and(s >= turns + 2, s < 2 * turns))
        def _():
            for way in range(2):
                h_copy(s - turns - 2, h, way).wait_recv()
                h_copy(s - turns - 1, h, way).start()

        @pl.when(s == 2 * turns)
        def _():
            for way in range(2):
                h_copy(turns - 2, h, way).wait_recv()
                h_last(h, way).start()

        @pl.when(s == 2 * turns + 1)
        def _():
            for way in range(2):
                h_last(h, way).wait_recv()

        return carry

    advances = 2 * (2 * turns + 2)

    def pair_copy():
        return remote(give, take, pair_send, pair_recv, sibling)

    def w_copy(j):
        return remote(w_give.at[j], w_take.at[j], w_send.at[j], w_recv.at[j], sibling)

    half = 2 * batch

    def x_copy(j, kind):
        if kind == 0:
            src, dst = part.at[j, 2, pl.ds(0, half)], relay.at[j, 0]
        elif kind == 1:
            src, dst = part.at[j, 2, pl.ds(half, half)], relay.at[j, 1]
        elif kind == 2:
            src, dst = part.at[j, 1], from_x.at[j, 0]
        else:
            src, dst = part.at[j, 3], from_x.at[j, 1]
        where = along(y_first(j), 3 if kind % 2 else 1)
        return remote(src, dst, x_send.at[kind, j], x_recv.at[kind, j], where)

    def y_copy(j, kind):
        where = along(1 - y_first(j), kind + 1)
        src = part.at[j, 0, pl.ds((kind + 1) * batch, batch)]
        return remote(src, from_y.at[j, kind], y_send.at[kind, j], y_recv.at[kind, j], where)

    pair_copy().start()

    def w_start(j, carry):
        w_copy(j).start()
        return carry

    lax.fori_loop(0, chunks, w_start, 0)
    pair_copy().wait_recv()
    for n in range(2):
        blocks = [q * ny + p for q in range(nx) for p in range(ny)]
        if n:
            blocks = [q * ny + p for p in range(ny) for q in range(nx)]
        own = jnp.concatenate([left[k * batch : (k + 1) * batch] for k in blocks], axis=0)
        pair = jnp.concatenate([take[k] for k in blocks], axis=0)
        lhs[n, :, :128] = own.astype(BF16)
        lhs[n, :, 128:] = pair.astype(BF16)
    lead_s2, lead_y, lead_end = ahead, ahead + 3, ahead + 6
    slots = groups * CAP
    shard = swap.shape[1]

    def first_advance(i):
        return jnp.minimum(2 + (4 * (jnp.minimum(i, ahead + chunks) - ahead)) // 3, advances)

    def multiply(i, carry):
        w_copy(i).wait_recv()
        right[i, :, 128:] = w_take[i].astype(BF16)
        product = lax.dot_general(
            lhs[y_first(i)],
            right[i],
            (((1,), (1,)), ((), ())),
            preferred_element_type=F32,
        )
        part[i] = product.reshape(part.shape[1:])
        x_copy(i, 0).start()
        x_copy(i, 1).start()
        return carry

    lax.fori_loop(0, ahead, multiply, 0)

    spare = tower.shape[0] - columns
    every = spread[...].reshape(groups * batch, 128)
    tower[pl.ds(columns, spare), :] = jnp.where(
        lax.broadcasted_iota(jnp.int32, (spare, 128), 0) == 0,
        jnp.broadcast_to(jnp.sum(every, axis=0, keepdims=True), (spare, 128)),
        0.0,
    )
    turned = every.T.astype(BF16)
    load.wait()
    for j in range(chunks):
        flat = jnp.dot(
            turned, pooled[:, j * CHUNK : (j + 1) * CHUNK], preferred_element_type=F32
        )
        tower[j * CHUNK : (j + 1) * CHUNK, :] = flat.T
    lax.fori_loop(0, 2, advance, 0)

    def step(i, carry):
        @pl.when(i < chunks)
        def _():
            multiply(i, 0)

        @pl.when(jnp.logical_and(i >= lead_s2, i < chunks + lead_s2))
        def _():
            j = i - lead_s2
            x_copy(j, 0).wait_recv()
            part[j, 1, pl.ds(0, half)] = part[j, 1, pl.ds(0, half)] + relay[j, 0]
            x_copy(j, 2).start()
            x_copy(j, 1).wait_recv()
            part[j, 3, pl.ds(half, half)] = part[j, 3, pl.ds(half, half)] + relay[j, 1]
            x_copy(j, 3).start()

        lax.fori_loop(first_advance(i), first_advance(i + 1), advance, 0)

        @pl.when(i == 5)
        def _():
            placing[...] = place_rows(ids_ref[pl.ds(me, 1), :], groups, local_rows)

        @pl.when(i == 6)
        def _():
            wide = jnp.broadcast_to(landing_rows(ids_ref[...], me, local_rows), (slots, 128))
            target[...] = wide.T[0:8].astype(jnp.int32)

        @pl.when(jnp.logical_and(i >= 7, i < 7 + nz))
        def _():
            n = i - 7
            k = turns + jnp.where(lax.rem(n, 2) == 0, (n + 1) // 2, -((n + 1) // 2))
            rows = lax.broadcasted_iota(jnp.int32, (shard, slots), 0)
            for low in range(2):
                owned = 1 - at_low if low == 0 else at_low
                hit = rows + (away(k) * 2 + owned) * shard == target[0:1]
                landing[n, pl.ds(low * shard, shard), :] = hit.astype(F32).astype(BF16)

        @pl.when(jnp.logical_and(i >= lead_y, i < chunks + lead_y))
        def _():
            j = i - lead_y
            x_copy(j, 2).wait_recv()
            x_copy(j, 3).wait_recv()
            part[j, 0] = part[j, 0] + from_x[j, 0] + from_x[j, 1]
            for kind in (1, 0, 2):
                y_copy(j, kind).start()

        @pl.when(i >= lead_end)
        def _():
            j = i - lead_end
            for kind in range(3):
                y_copy(j, kind).wait_recv()
            total = part[j, 0, pl.ds(0, batch)] + from_y[j, 0] + from_y[j, 1] + from_y[j, 2]
            for n in range(CHUNK // 128):
                grads[j * (CHUNK // 128) + n] = total[:, n * 128 : (n + 1) * 128]

        return carry

    lax.fori_loop(ahead, chunks + lead_end, step, 0)

    wide = halves(grads[...].reshape(-1, 128))
    both = jnp.dot(placing[...], wide, preferred_element_type=F32)
    out_rows[...] = (both[:, :128] + both[:, 128:]).reshape(out_rows.shape)

    def a_copy(k):
        owner = lax.rem(me + k, groups)
        return remote(
            out_rows.at[owner], in_rows.at[me], a_send.at[k], a_recv.at[k], {"emb": owner}
        )

    def a_start(k, carry):
        a_copy(lax.rem(k + 14, groups - 1) + 1).start()
        return carry

    lax.fori_loop(1, groups, a_start, 0)
    in_rows[me] = out_rows[me]
    lax.fori_loop(first_advance(chunks + lead_end), advances, advance, 0)

    def a_wait(k, carry):
        a_copy(k).wait_recv()
        return carry

    lax.fori_loop(1, groups, a_wait, 0)

    tower_out = pltpu.make_async_copy(t_final, tower_ref, out_sem)
    tower_out.start()

    hop = turns // 2
    reach = turns - hop
    cut = shard // 16 * 8
    order = sorted(range(nz), key=lambda k: (-min(k, nz - k), k))
    near = order[2 * reach - 1 :]
    wide = halves(in_rows[...].reshape(slots, 128))

    def s_copy(n, k):
        return remote(
            sums.at[n, pl.ds(0, shard)], swap.at[k], s_send.at[k], s_recv.at[k], partner
        )

    def q_copy(side, j):
        k = hop + j if side == 0 else nz - hop - j
        if j == reach:
            rows = pl.ds(0, cut) if side == 0 else pl.ds(cut, shard - cut)
            src, dst = mixed.at[k, rows], merge.at[side, j, rows]
        else:
            src, dst = mixed.at[k], merge.at[side, j]
        return remote(
            src, dst, q_send.at[side, j], q_recv.at[side, j], peer(j if side == 0 else nz - j)
        )

    def z_copy(k):
        return remote(mixed.at[k], from_z.at[k], z_send.at[k], z_recv.at[k], peer(k))

    def g_copy(k):
        place = final.at[replica]
        return remote(place, place, g_send.at[k], g_recv.at[k], peer(k))

    def e_copy(side, j):
        place = final.at[away(nz - hop if side == 0 else hop) * 2 + at_low]
        if j == reach:
            place = place.at[pl.ds(0, cut) if side == 0 else pl.ds(cut, shard - cut)]
        return remote(
            place, place, e_send.at[side, j], e_recv.at[side, j], peer(j if side == 0 else nz - j)
        )

    def f_copy(k):
        place = final.at[away(nz - k) * 2 + at_low]
        return remote(place, place, f_send.at[k], f_recv.at[k], partner)

    parts = 3 if nz % 3 == 0 else 2
    size = nz // parts
    for n in range(parts):
        both = jnp.dot(
            landing[n * size : (n + 1) * size].reshape(size * 2 * shard, slots),
            wide,
            preferred_element_type=F32,
        )
        sums[n * size : (n + 1) * size] = (both[:, :128] + both[:, 128:]).reshape(
            size, 2 * shard, 128
        )
        for m in range(n * size, (n + 1) * size):
            s_copy(m, order[m]).start()

    for n, k in enumerate(order):
        s_copy(n, k).wait_recv()
        mixed[k] = sums[n, pl.ds(shard, shard), :] + swap[k]
        if k == turns:
            q_copy(0, reach).start()
            q_copy(1, reach).start()
        elif hop < k < turns:
            q_copy(0, k - hop).start()
        elif turns < k < nz - hop:
            q_copy(1, nz - hop - k).start()
        elif k not in (0, hop, nz - hop):
            z_copy(k).start()
        if n == max(2 * reach, nz - 4):
            for side in range(2):
                mid = (hop, nz - hop)[side]
                for j in range(reach, 0, -1):
                    q_copy(side, j).wait_recv()
                    if j == reach:
                        rows = pl.ds(0, cut) if side == 0 else pl.ds(cut, shard - cut)
                        mixed[mid, rows] = mixed[mid, rows] + merge[side, j, rows]
                    else:
                        mixed[mid] = mixed[mid] + merge[side, j]
                z_copy(mid).start()
    total = mixed[0]
    for k in near[::-1]:
        if k:
            z_copy(k).wait_recv()
            total = total + from_z[k]
    final[replica] = total
    for k in near:
        if k:
            g_copy(k).start()
    f_copy(0).start()
    for side in range(2):
        mid = (hop, nz - hop)[side]
        g_copy(mid).wait_recv()
        for j in range(reach, 0, -1):
            e_copy(side, j).start()
        f_copy(mid).start()

    def drain(j, carry):
        w_copy(j).wait_send()
        for kind in range(4):
            x_copy(j, kind).wait_send()
        for kind in range(3):
            y_copy(j, kind).wait_send()
        return carry

    def a_drain(k, carry):
        a_copy(k).wait_send()
        return carry

    def t_drain(h, carry):
        for way in range(2):
            r_first(h, way).wait_send()
            h_last(h, way).wait_send()
            h_copy(0, h, way).wait_send()
        b_copy(h).wait_send()

        def inner(s, carry):
            for way in range(2):
                r_copy(s, h, way).wait_send()
            return carry

        def inner_h(s, carry):
            for way in range(2):
                h_copy(s, h, way).wait_send()
            return carry

        lax.fori_loop(1, turns, inner, 0)
        lax.fori_loop(1, turns - 1, inner_h, 0)
        return carry

    pair_copy().wait_send()
    lax.fori_loop(0, chunks, drain, 0)
    lax.fori_loop(1, groups, a_drain, 0)
    lax.fori_loop(0, 2, t_drain, 0)
    for k in near[::-1]:
        if k not in (0, hop, nz - hop):
            g_copy(k).wait_recv()
            f_copy(k).start()
    for j in range(1, reach):
        for side in range(2):
            e_copy(side, j).wait_recv()
            f_copy(hop + j if side == 0 else nz - hop - j).start()
    e_copy(0, reach).wait_recv()
    e_copy(1, reach).wait_recv()
    f_copy(turns).start()
    for k in order[::-1]:
        f_copy(k).wait_recv()
    for n, k in enumerate(order):
        s_copy(n, k).wait_send()
        f_copy(k).wait_send()
        if k and k in near:
            z_copy(k).wait_send()
            g_copy(k).wait_send()
    for side in range(2):
        for j in range(1, reach + 1):
            q_copy(side, j).wait_send()
            e_copy(side, j).wait_send()
    tower_out.wait()
    total_ref[...] = final[...]


def finish_kernel(
    total_hbm,
    tower_hbm,
    table_ref,
    accum_ref,
    weight_ref,
    new_table_ref,
    new_accum_ref,
    bias_ref,
    total_ref,
    tower_ref,
    sems,
):
    columns = weight_ref.shape[0]
    local_rows = table_ref.shape[0]
    piece = columns // 4
    half = local_rows // 2
    loads, outs = [], []
    for n in range(4):
        rows = pl.ds(n * piece, piece + 8 if n == 3 else piece)
        loads.append(pltpu.make_async_copy(tower_hbm.at[rows], tower_ref.at[rows], sems.at[n]))
        rows = pl.ds(n * piece, piece)
        outs.append(pltpu.make_async_copy(tower_ref.at[rows], weight_ref.at[rows], sems.at[4 + n]))
    for n in range(2):
        rows = pl.ds(n * half, half)
        loads.append(pltpu.make_async_copy(total_hbm.at[rows], total_ref.at[rows], sems.at[8 + n]))
    for load in loads:
        load.start()
    diagonal = lax.broadcasted_iota(jnp.int32, (128, 128), 0) == lax.broadcasted_iota(
        jnp.int32, (128, 128), 1
    )
    ones = jnp.ones((128, 128), F32)
    for load, out in zip(loads, outs):
        load.wait()
        out.start()
    for load in loads[4:]:
        load.wait()
    bias_ref[...] = tower_ref[pl.ds(columns, 1), :]
    for n in range(accum_ref.shape[0]):
        rows = pl.ds(n * 128, 128)
        row_grad = total_ref[rows, :]
        terms = row_grad * row_grad * (1.0 / 128.0) + jnp.where(
            diagonal, jnp.broadcast_to(accum_ref[n : n + 1, :], (128, 128)), 0.0
        )
        grown = jnp.dot(terms, ones, precision=lax.Precision.HIGHEST, preferred_element_type=F32)
        new_table_ref[rows, :] = table_ref[rows, :] - learn_rate * row_grad / jnp.sqrt(grown)
        new_accum_ref[n : n + 1, :] = jnp.sum(
            jnp.where(diagonal, grown, 0.0), axis=0, keepdims=True
        )
    for out in outs:
        out.wait()


def finish(total, tower, table, accum, columns):
    vmem = pltpu.VMEM
    return pl.pallas_call(
        finish_kernel,
        out_shape=(
            jax.ShapeDtypeStruct((columns, 128), F32),
            jax.ShapeDtypeStruct(table.shape, F32),
            jax.ShapeDtypeStruct(accum.shape, F32),
            jax.ShapeDtypeStruct((1, 128), F32),
        ),
        in_specs=[pl.BlockSpec(memory_space=pl.ANY)] * 2 + [pl.BlockSpec(memory_space=vmem)] * 2,
        out_specs=[pl.BlockSpec(memory_space=pl.ANY)] + [pl.BlockSpec(memory_space=vmem)] * 3,
        scratch_shapes=[
            vmem(table.shape, F32),
            vmem((columns + 8, 128), F32),
            pltpu.SemaphoreType.DMA((10,)),
        ],
        compiler_params=pltpu.CompilerParams(vmem_limit_bytes=58 << 20),
    )(total, tower, table, accum)


def step(pooled, upstream, preact, tower_w, ids, local_rows, dense, ny, nx):
    samples = upstream.shape[0]
    groups = ny * nx * 2
    nz = dense // 2
    batch = samples // groups
    columns = tower_w.shape[0]
    chunks = columns // CHUNK
    entries = ids.shape[1]
    slots = groups * CAP
    shard = -(-local_rows // (dense * 8)) * 8
    piece = -(-(columns + 8) // (nz * 32)) * 16
    turns = nz // 2
    vmem = pltpu.VMEM
    dma = pltpu.SemaphoreType.DMA
    total, tower = pl.pallas_call(
        functools.partial(step_kernel, ny, nx, nz, local_rows),
        out_shape=(
            jax.ShapeDtypeStruct((dense, shard, 128), F32),
            jax.ShapeDtypeStruct((nz * 2 * piece, 128), F32),
        ),
        in_specs=[pl.BlockSpec(memory_space=pl.ANY)] + [pl.BlockSpec(memory_space=vmem)] * 4,
        out_specs=[pl.BlockSpec(memory_space=vmem), pl.BlockSpec(memory_space=pl.ANY)],
        scratch_shapes=[
            vmem(pooled.shape, BF16),
            vmem((groups, batch, 128), F32),
            vmem((nx * ny, batch, 128), F32),
            vmem((nx * ny, batch, 128), F32),
            vmem((chunks, CHUNK, 128), F32),
            vmem((chunks, CHUNK, 128), F32),
            vmem((nx * ny * batch, 128), F32),
            vmem((2, nx * ny * batch, 256), BF16),
            vmem((chunks, CHUNK, 256), BF16),
            vmem((chunks, nx, ny * batch, CHUNK), F32),
            vmem((chunks, 2, 2 * batch, CHUNK), F32),
            vmem((chunks, 2, ny * batch, CHUNK), F32),
            vmem((chunks, 3, batch, CHUNK), F32),
            vmem((columns // 128, batch, 128), F32),
            vmem((slots, entries), BF16),
            vmem((groups, CAP, 128), F32),
            vmem((groups, CAP, 128), F32),
            vmem((8, slots), jnp.int32),
            vmem((nz, 2 * shard, slots), BF16),
            vmem((nz, 2 * shard, 128), F32),
            vmem((nz, shard, 128), F32),
            vmem((nz, shard, 128), F32),
            vmem((nz, shard, 128), F32),
            vmem((2, turns - turns // 2 + 1, shard, 128), F32),
            vmem((dense, shard, 128), F32),
            vmem((nz * 2 * piece, 128), F32),
            vmem((2, turns, 2, piece, 128), F32),
            vmem((2, piece, 128), F32),
            vmem((nz * 2 * piece, 128), F32),
            dma,
            dma,
            dma((chunks,)),
            dma((chunks,)),
            dma((4, chunks)),
            dma((4, chunks)),
            dma((3, chunks)),
            dma((3, chunks)),
            dma((groups,)),
            dma((groups,)),
        ]
        + [dma((nz,))] * 8
        + [
            dma((2, turns, 2)),
            dma((2, turns, 2)),
            dma((2,)),
            dma((2,)),
            dma((2, turns, 2)),
            dma((2, turns, 2)),
        ]
        + [dma((2, turns - turns // 2 + 1))] * 4
        + [dma, dma],
        compiler_params=pltpu.CompilerParams(
            collective_id=0, has_side_effects=True, vmem_limit_bytes=58 << 20
        ),
        cost_estimate=pl.CostEstimate(flops=1 << 30, bytes_accessed=8 << 20, transcendentals=0),
    )(pooled, upstream, preact, tower_w, ids)
    return total.reshape(dense * shard, 128), tower


def shards(pooled, upstream, preact, tower_w, row_ids, table, accum):
    groups = lax.axis_size("emb")
    dense = lax.axis_size("dense")
    local_rows = table.shape[0]
    ids = row_ids.reshape(groups, -1, row_ids.shape[1]).transpose(0, 2, 1).reshape(groups, -1)
    total, tower = step(
        pooled, upstream, preact, tower_w, ids, local_rows, dense, 4, 4
    )
    columns = tower_w.shape[0]
    weight_grad, new_table, new_accum, bias_grad = finish(
        total, tower, table, accum.reshape(-1, 128), columns
    )
    return (weight_grad, bias_grad.reshape(-1), new_table, new_accum.reshape(-1))


def solution(mesh):
    placed = (
        P("dense", None),
        P("dense", "emb"),
        P("dense", "emb"),
        P(None, "emb"),
        P("dense", None),
        P("emb", None),
        P("emb"),
    )
    return jax.shard_map(
        shards,
        mesh=mesh,
        in_specs=placed,
        out_specs=(P(None, "emb"), P("emb"), P("emb", None), P("emb")),
        check_vma=False,
    )
```

```python
import functools

import jax
import jax.numpy as jnp
from jax import lax
from jax.experimental import pallas as pl
from jax.experimental.pallas import tpu as pltpu
from jax.sharding import PartitionSpec as P

learn_rate = 0.5
MESH = pl.DeviceIdType.MESH
CHUNK = 256
CAP = 40
F32 = jnp.float32
BF16 = jnp.bfloat16


def silu_slope(preact_f):
    sigmoid_val = jax.nn.sigmoid(preact_f)
    return sigmoid_val * (1.0 + preact_f * (1.0 - sigmoid_val))


def remote(src, dst, send, recv, where):
    return pltpu.make_async_remote_copy(
        src_ref=src, dst_ref=dst, send_sem=send, recv_sem=recv, device_id=where, device_id_type=MESH
    )


def place_rows(ids, groups, local_rows):
    entries = ids.shape[1]
    owners = ids // local_rows
    member = (lax.broadcasted_iota(jnp.int32, (groups, entries), 0) == owners).astype(F32)
    earlier = (
        lax.broadcasted_iota(jnp.int32, (entries, entries), 0)
        < lax.broadcasted_iota(jnp.int32, (entries, entries), 1)
    ).astype(F32).astype(BF16)
    prior = jnp.dot(member.astype(BF16), earlier, preferred_element_type=F32)
    ranks = jnp.sum(prior * member, axis=0, keepdims=True).astype(jnp.int32)
    slot_of = owners * CAP + ranks
    return (
        (lax.broadcasted_iota(jnp.int32, (groups * CAP, entries), 0) == slot_of)
        .astype(F32)
        .astype(BF16)
    )


def halves(rows):
    high = rows.astype(BF16)
    low = (rows - high.astype(F32)).astype(BF16)
    return jnp.concatenate([high, low], axis=1)


def landing_rows(ids, mine, local_rows):
    blocks, entries = ids.shape
    owners = ids // local_rows
    member = (owners == mine).astype(F32)
    earlier = (
        lax.broadcasted_iota(jnp.int32, (entries, entries), 0)
        < lax.broadcasted_iota(jnp.int32, (entries, entries), 1)
    ).astype(F32).astype(BF16)
    prior = jnp.dot(member.astype(BF16), earlier, preferred_element_type=F32)
    ranks = jnp.where(member > 0.5, prior.astype(jnp.int32), -1)
    offsets = (ids - owners * local_rows + 1).astype(F32)
    slots = lax.broadcasted_iota(jnp.int32, (CAP, entries), 0)
    columns = []
    for block in range(blocks):
        hit = jnp.where(slots == ranks[block : block + 1], offsets[block : block + 1], 0.0)
        columns.append(jnp.sum(hit, axis=1, keepdims=True))
    return jnp.concatenate(columns, axis=0) - 1.0


def step_kernel(
    ny,
    nx,
    nz,
    local_rows,
    pooled_ref,
    upstream_ref,
    preact_ref,
    w_ref,
    ids_ref,
    total_ref,
    tower_ref,
    pooled,
    spread,
    give,
    take,
    w_give,
    w_take,
    left,
    lhs,
    right,
    part,
    relay,
    from_x,
    from_y,
    grads,
    placing,
    out_rows,
    in_rows,
    target,
    landing,
    sums,
    swap,
    mixed,
    from_z,
    merge,
    final,
    tower,
    t_from,
    t_swap,
    t_final,
    pair_send,
    pair_recv,
    w_send,
    w_recv,
    x_send,
    x_recv,
    y_send,
    y_recv,
    a_send,
    a_recv,
    s_send,
    s_recv,
    z_send,
    z_recv,
    g_send,
    g_recv,
    f_send,
    f_recv,
    r_send,
    r_recv,
    b_send,
    b_recv,
    h_send,
    h_recv,
    q_send,
    q_recv,
    e_send,
    e_recv,
    in_sem,
    out_sem,
):
    chunks = part.shape[0]
    groups = ny * nx * 2
    batch = upstream_ref.shape[0] // groups
    columns = w_ref.shape[0]
    me = lax.axis_index("emb")
    core = lax.rem(me, 2)
    at_x = lax.rem(me // 2, nx)
    at_y = me // (2 * nx)
    replica = lax.axis_index("dense")
    at_low = lax.rem(replica, 2)
    at_z = replica // 2

    def there(y, x, c):
        return {"emb": (lax.rem(y, ny) * nx + lax.rem(x, nx)) * 2 + c}

    sibling = there(at_y, at_x, 1 - core)

    ahead = 4

    def y_first(j):
        return lax.rem(j, 2) * ((chunks + ahead - 1 - j) // chunks)

    def along(turned, k):
        return there(at_y + turned * k, at_x + (1 - turned) * k, core)

    partner = {"dense": at_z * 2 + 1 - at_low}

    def away(k):
        return lax.rem(at_z + k, nz)

    def peer(k):
        return {"dense": away(k) * 2 + at_low}

    z_ends = (peer(1), peer(nz - 1))

    load = pltpu.make_async_copy(pooled_ref, pooled, in_sem)
    load.start()
    barrier = pltpu.get_barrier_semaphore()

    def greet(k, carry):
        pl.semaphore_signal(
            barrier, inc=1, device_id={"emb": lax.rem(me + k, groups)}, device_id_type=MESH
        )
        return carry

    def greet_z(k, carry):
        pl.semaphore_signal(barrier, inc=1, device_id=peer(k), device_id_type=MESH)
        return carry

    lax.fori_loop(1, groups, greet, 0)
    lax.fori_loop(1, nz, greet_z, 0)
    pl.semaphore_signal(barrier, inc=1, device_id=partner, device_id_type=MESH)

    slope = silu_slope(preact_ref[...].astype(F32))
    deltas = (upstream_ref[...].astype(F32) * slope).astype(BF16).astype(F32)
    spread[...] = deltas.reshape(groups, batch, 128)
    for q in range(nx):
        for p in range(ny):
            block = (lax.rem(at_y + p, ny) * nx + lax.rem(at_x + q, nx)) * 2
            give[q * ny + p] = spread[block + 1 - core]
            left[pl.ds((q * ny + p) * batch, batch), :] = spread[block + core]
    w_give[...] = w_ref[...].astype(F32).reshape(w_give.shape)
    right[:, :, :128] = w_ref[...].reshape(chunks, CHUNK, 128)

    pl.semaphore_wait(barrier, groups - 1 + nz)

    turns = nz // 2
    part_rows = t_swap.shape[1]
    bit = part_rows // 2

    def stretch(t, h, first=0, size=part_rows):
        return pl.ds(pl.multiple_of((t * 2 + h) * part_rows + first, 8), size)

    def ring_at(way, k):
        return away(k) if way == 0 else away(nz - k)

    def r_copy(s, h, way):
        return remote(
            tower.at[stretch(ring_at(way, turns - s), h)],
            t_from.at[way, s, h],
            r_send.at[way, s, h],
            r_recv.at[way, s, h],
            z_ends[way],
        )

    def r_first(h, way):
        rows = pl.ds(way * bit, bit)
        return remote(
            tower.at[stretch(away(turns), h, way * bit, bit)],
            t_from.at[way, 0, h, rows],
            r_send.at[way, 0, h],
            r_recv.at[way, 0, h],
            z_ends[way],
        )

    def b_copy(h):
        place = tower.at[stretch(at_z, h)]
        return remote(place, t_swap.at[h], b_send.at[h], b_recv.at[h], partner)

    def h_copy(s, h, way):
        place = t_final.at[stretch(ring_at(1 - way, s), h)]
        return remote(place, place, h_send.at[way, s, h], h_recv.at[way, s, h], z_ends[way])

    def h_last(h, way):
        place = t_final.at[stretch(ring_at(1 - way, turns - 1), h, way * bit, bit)]
        return remote(
            place,
            place,
            h_send.at[way, turns - 1, h],
            h_recv.at[way, turns - 1, h],
            z_ends[way],
        )

    def advance(n, carry):
        h = lax.rem(n, 2)
        s = n // 2

        @pl.when(s == 0)
        def _():
            for way in range(2):
                r_first(h, way).start()

        @pl.when(s == 1)
        def _():
            for way in range(2):
                r_first(h, way).wait_recv()
                t = ring_at(way, turns - 1)
                rows = pl.ds(way * bit, bit)
                here = stretch(t, h, way * bit, bit)
                tower[here, :] = tower[here, :] + t_from[way, 0, h, rows]
                r_copy(1, h, way).start()

        @pl.when(jnp.logical_and(s >= 2, s < turns))
        def _():
            for way in range(2):
                r_copy(s - 1, h, way).wait_recv()
                t = ring_at(way, turns - s)
                tower[stretch(t, h), :] = tower[stretch(t, h), :] + t_from[way, s - 1, h]
                r_copy(s, h, way).start()

        @pl.when(s == turns)
        def _():
            r_copy(turns - 1, h, 0).wait_recv()
            r_copy(turns - 1, h, 1).wait_recv()
            here = stretch(at_z, h)
            tower[here, :] = (
                tower[here, :] + t_from[0, turns - 1, h] + t_from[1, turns - 1, h]
            )
            b_copy(h).start()

        @pl.when(s == turns + 1)
        def _():
            b_copy(h).wait_recv()
            t_final[stretch(at_z, h), :] = tower[stretch(at_z, h), :] + t_swap[h]
            for way in range(2):
                h_copy(0, h, way).start()

        @pl.when(jnp.logical_and(s >= turns + 2, s < 2 * turns))
        def _():
            for way in range(2):
                h_copy(s - turns - 2, h, way).wait_recv()
                h_copy(s - turns - 1, h, way).start()

        @pl.when(s == 2 * turns)
        def _():
            for way in range(2):
                h_copy(turns - 2, h, way).wait_recv()
                h_last(h, way).start()

        @pl.when(s == 2 * turns + 1)
        def _():
            for way in range(2):
                h_last(h, way).wait_recv()

        return carry

    advances = 2 * (2 * turns + 2)

    def pair_copy():
        return remote(give, take, pair_send, pair_recv, sibling)

    def w_copy(j):
        return remote(w_give.at[j], w_take.at[j], w_send.at[j], w_recv.at[j], sibling)

    half = 2 * batch

    def x_copy(j, kind):
        if kind == 0:
            src, dst = part.at[j, 2, pl.ds(0, half)], relay.at[j, 0]
        elif kind == 1:
            src, dst = part.at[j, 2, pl.ds(half, half)], relay.at[j, 1]
        elif kind == 2:
            src, dst = part.at[j, 1], from_x.at[j, 0]
        else:
            src, dst = part.at[j, 3], from_x.at[j, 1]
        where = along(y_first(j), 3 if kind % 2 else 1)
        return remote(src, dst, x_send.at[kind, j], x_recv.at[kind, j], where)

    def y_copy(j, kind):
        where = along(1 - y_first(j), kind + 1)
        src = part.at[j, 0, pl.ds((kind + 1) * batch, batch)]
        return remote(src, from_y.at[j, kind], y_send.at[kind, j], y_recv.at[kind, j], where)

    pair_copy().start()

    def w_start(j, carry):
        w_copy(j).start()
        return carry

    lax.fori_loop(0, chunks, w_start, 0)
    pair_copy().wait_recv()
    for n in range(2):
        blocks = [q * ny + p for q in range(nx) for p in range(ny)]
        if n:
            blocks = [q * ny + p for p in range(ny) for q in range(nx)]
        own = jnp.concatenate([left[k * batch : (k + 1) * batch] for k in blocks], axis=0)
        pair = jnp.concatenate([take[k] for k in blocks], axis=0)
        lhs[n, :, :128] = own.astype(BF16)
        lhs[n, :, 128:] = pair.astype(BF16)
    lead_s2, lead_y, lead_end = ahead, ahead + 3, ahead + 6
    slots = groups * CAP
    shard = swap.shape[1]

    def first_advance(i):
        return jnp.minimum(2 + (4 * (jnp.minimum(i, ahead + chunks) - ahead)) // 3, advances)

    def multiply(i, carry):
        w_copy(i).wait_recv()
        right[i, :, 128:] = w_take[i].astype(BF16)
        product = lax.dot_general(
            lhs[y_first(i)],
            right[i],
            (((1,), (1,)), ((), ())),
            preferred_element_type=F32,
        )
        part[i] = product.reshape(part.shape[1:])
        x_copy(i, 0).start()
        x_copy(i, 1).start()
        return carry

    lax.fori_loop(0, ahead, multiply, 0)

    spare = tower.shape[0] - columns
    every = spread[...].reshape(groups * batch, 128)
    tower[pl.ds(columns, spare), :] = jnp.where(
        lax.broadcasted_iota(jnp.int32, (spare, 128), 0) == 0,
        jnp.broadcast_to(jnp.sum(every, axis=0, keepdims=True), (spare, 128)),
        0.0,
    )
    turned = every.T.astype(BF16)
    load.wait()
    for j in range(chunks):
        flat = jnp.dot(
            turned, pooled[:, j * CHUNK : (j + 1) * CHUNK], preferred_element_type=F32
        )
        tower[j * CHUNK : (j + 1) * CHUNK, :] = flat.T
    lax.fori_loop(0, 2, advance, 0)

    def step(i, carry):
        @pl.when(i < chunks)
        def _():
            multiply(i, 0)

        @pl.when(jnp.logical_and(i >= lead_s2, i < chunks + lead_s2))
        def _():
            j = i - lead_s2
            x_copy(j, 0).wait_recv()
            part[j, 1, pl.ds(0, half)] = part[j, 1, pl.ds(0, half)] + relay[j, 0]
            x_copy(j, 2).start()
            x_copy(j, 1).wait_recv()
            part[j, 3, pl.ds(half, half)] = part[j, 3, pl.ds(half, half)] + relay[j, 1]
            x_copy(j, 3).start()

        lax.fori_loop(first_advance(i), first_advance(i + 1), advance, 0)

        @pl.when(i == 5)
        def _():
            placing[...] = place_rows(ids_ref[pl.ds(me, 1), :], groups, local_rows)

        @pl.when(i == 6)
        def _():
            wide = jnp.broadcast_to(landing_rows(ids_ref[...], me, local_rows), (slots, 128))
            target[...] = wide.T[0:8].astype(jnp.int32)

        @pl.when(jnp.logical_and(i >= 7, i < 7 + nz))
        def _():
            n = i - 7
            k = turns + jnp.where(lax.rem(n, 2) == 0, (n + 1) // 2, -((n + 1) // 2))
            rows = lax.broadcasted_iota(jnp.int32, (shard, slots), 0)
            for low in range(2):
                owned = 1 - at_low if low == 0 else at_low
                hit = rows + (away(k) * 2 + owned) * shard == target[0:1]
                landing[n, pl.ds(low * shard, shard), :] = hit.astype(F32).astype(BF16)

        @pl.when(jnp.logical_and(i >= lead_y, i < chunks + lead_y))
        def _():
            j = i - lead_y
            x_copy(j, 2).wait_recv()
            x_copy(j, 3).wait_recv()
            part[j, 0] = part[j, 0] + from_x[j, 0] + from_x[j, 1]
            for kind in (1, 0, 2):
                y_copy(j, kind).start()

        @pl.when(i >= lead_end)
        def _():
            j = i - lead_end
            for kind in range(3):
                y_copy(j, kind).wait_recv()
            total = part[j, 0, pl.ds(0, batch)] + from_y[j, 0] + from_y[j, 1] + from_y[j, 2]
            for n in range(CHUNK // 128):
                grads[j * (CHUNK // 128) + n] = total[:, n * 128 : (n + 1) * 128]

        return carry

    lax.fori_loop(ahead, chunks + lead_end, step, 0)

    wide = halves(grads[...].reshape(-1, 128))
    both = jnp.dot(placing[...], wide, preferred_element_type=F32)
    out_rows[...] = (both[:, :128] + both[:, 128:]).reshape(out_rows.shape)

    def a_copy(k):
        owner = lax.rem(me + k, groups)
        return remote(
            out_rows.at[owner], in_rows.at[me], a_send.at[k], a_recv.at[k], {"emb": owner}
        )

    def a_start(k, carry):
        a_copy(lax.rem(k + 14, groups - 1) + 1).start()
        return carry

    lax.fori_loop(1, groups, a_start, 0)
    in_rows[me] = out_rows[me]
    lax.fori_loop(first_advance(chunks + lead_end), advances, advance, 0)

    def a_wait(k, carry):
        a_copy(k).wait_recv()
        return carry

    lax.fori_loop(1, groups, a_wait, 0)

    tower_out = pltpu.make_async_copy(t_final, tower_ref, out_sem)
    tower_out.start()

    hop = turns // 2
    reach = turns - hop
    cut = shard // 16 * 8
    order = sorted(range(nz), key=lambda k: (-min(k, nz - k), k))
    near = order[2 * reach - 1 :]
    wide = halves(in_rows[...].reshape(slots, 128))

    def s_copy(n, k):
        return remote(
            sums.at[n, pl.ds(0, shard)], swap.at[k], s_send.at[k], s_recv.at[k], partner
        )

    def q_copy(side, j):
        k = hop + j if side == 0 else nz - hop - j
        if j == reach:
            rows = pl.ds(0, cut) if side == 0 else pl.ds(cut, shard - cut)
            src, dst = mixed.at[k, rows], merge.at[side, j, rows]
        else:
            src, dst = mixed.at[k], merge.at[side, j]
        return remote(
            src, dst, q_send.at[side, j], q_recv.at[side, j], peer(j if side == 0 else nz - j)
        )

    def z_copy(k):
        return remote(mixed.at[k], from_z.at[k], z_send.at[k], z_recv.at[k], peer(k))

    def g_copy(k):
        place = final.at[replica]
        return remote(place, place, g_send.at[k], g_recv.at[k], peer(k))

    def e_copy(side, j):
        place = final.at[away(nz - hop if side == 0 else hop) * 2 + at_low]
        if j == reach:
            place = place.at[pl.ds(0, cut) if side == 0 else pl.ds(cut, shard - cut)]
        return remote(
            place, place, e_send.at[side, j], e_recv.at[side, j], peer(j if side == 0 else nz - j)
        )

    def f_copy(k):
        place = final.at[away(nz - k) * 2 + at_low]
        return remote(place, place, f_send.at[k], f_recv.at[k], partner)

    parts = 3 if nz % 3 == 0 else 2
    size = nz // parts
    for n in range(parts):
        both = jnp.dot(
            landing[n * size : (n + 1) * size].reshape(size * 2 * shard, slots),
            wide,
            preferred_element_type=F32,
        )
        sums[n * size : (n + 1) * size] = (both[:, :128] + both[:, 128:]).reshape(
            size, 2 * shard, 128
        )
        for m in range(n * size, (n + 1) * size):
            s_copy(m, order[m]).start()

    for n, k in enumerate(order):
        s_copy(n, k).wait_recv()
        mixed[k] = sums[n, pl.ds(shard, shard), :] + swap[k]
        if k == turns:
            q_copy(0, reach).start()
            q_copy(1, reach).start()
        elif hop < k < turns:
            q_copy(0, k - hop).start()
        elif turns < k < nz - hop:
            q_copy(1, nz - hop - k).start()
        elif k not in (0, hop, nz - hop):
            z_copy(k).start()
        if n == max(2 * reach, nz - 4):
            for side in range(2):
                mid = (hop, nz - hop)[side]
                for j in range(reach, 0, -1):
                    q_copy(side, j).wait_recv()
                    if j == reach:
                        rows = pl.ds(0, cut) if side == 0 else pl.ds(cut, shard - cut)
                        mixed[mid, rows] = mixed[mid, rows] + merge[side, j, rows]
                    else:
                        mixed[mid] = mixed[mid] + merge[side, j]
                z_copy(mid).start()
    total = mixed[0]
    for k in near[::-1]:
        if k:
            z_copy(k).wait_recv()
            total = total + from_z[k]
    final[replica] = total
    for k in near:
        if k:
            g_copy(k).start()
    f_copy(0).start()
    for side in range(2):
        mid = (hop, nz - hop)[side]
        g_copy(mid).wait_recv()
        for j in range(reach, 0, -1):
            e_copy(side, j).start()
        f_copy(mid).start()

    def drain(j, carry):
        w_copy(j).wait_send()
        for kind in range(4):
            x_copy(j, kind).wait_send()
        for kind in range(3):
            y_copy(j, kind).wait_send()
        return carry

    def a_drain(k, carry):
        a_copy(k).wait_send()
        return carry

    def t_drain(h, carry):
        for way in range(2):
            r_first(h, way).wait_send()
            h_last(h, way).wait_send()
            h_copy(0, h, way).wait_send()
        b_copy(h).wait_send()

        def inner(s, carry):
            for way in range(2):
                r_copy(s, h, way).wait_send()
            return carry

        def inner_h(s, carry):
            for way in range(2):
                h_copy(s, h, way).wait_send()
            return carry

        lax.fori_loop(1, turns, inner, 0)
        lax.fori_loop(1, turns - 1, inner_h, 0)
        return carry

    pair_copy().wait_send()
    lax.fori_loop(0, chunks, drain, 0)
    lax.fori_loop(1, groups, a_drain, 0)
    lax.fori_loop(0, 2, t_drain, 0)
    for k in near[::-1]:
        if k not in (0, hop, nz - hop):
            g_copy(k).wait_recv()
            f_copy(k).start()
    for j in range(1, reach):
        for side in range(2):
            e_copy(side, j).wait_recv()
            f_copy(hop + j if side == 0 else nz - hop - j).start()
    e_copy(0, reach).wait_recv()
    e_copy(1, reach).wait_recv()
    f_copy(turns).start()
    for k in order[::-1]:
        f_copy(k).wait_recv()
    for n, k in enumerate(order):
        s_copy(n, k).wait_send()
        f_copy(k).wait_send()
        if k and k in near:
            z_copy(k).wait_send()
            g_copy(k).wait_send()
    for side in range(2):
        for j in range(1, reach + 1):
            q_copy(side, j).wait_send()
            e_copy(side, j).wait_send()
    tower_out.wait()
    total_ref[...] = final[...]


def finish_kernel(
    total_hbm,
    tower_hbm,
    table_ref,
    accum_ref,
    weight_ref,
    new_table_hbm,
    new_accum_ref,
    bias_ref,
    total_ref,
    fresh,
    tower_ref,
    sems,
):
    columns = weight_ref.shape[0]
    local_rows = table_ref.shape[0]
    piece = columns // 4
    size = local_rows // 4
    towers, totals, weights, tables = [], [], [], []
    for n in range(4):
        rows = pl.ds(n * size, size)
        totals.append(pltpu.make_async_copy(total_hbm.at[rows], total_ref.at[rows], sems.at[n]))
        tables.append(pltpu.make_async_copy(fresh.at[rows], new_table_hbm.at[rows], sems.at[4 + n]))
        rows = pl.ds(n * piece, piece + 8 if n == 3 else piece)
        towers.append(pltpu.make_async_copy(tower_hbm.at[rows], tower_ref.at[rows], sems.at[8 + n]))
        rows = pl.ds(n * piece, piece)
        weights.append(
            pltpu.make_async_copy(tower_ref.at[rows], weight_ref.at[rows], sems.at[12 + n])
        )
    for n in range(4):
        totals[n].start()
        towers[n].start()
    diagonal = lax.broadcasted_iota(jnp.int32, (128, 128), 0) == lax.broadcasted_iota(
        jnp.int32, (128, 128), 1
    )
    ones = jnp.ones((128, 128), F32)
    for n in range(4):
        totals[n].wait()
        for m in range(n * size // 128, (n + 1) * size // 128):
            rows = pl.ds(m * 128, 128)
            row_grad = total_ref[rows, :]
            terms = row_grad * row_grad * (1.0 / 128.0) + jnp.where(
                diagonal, jnp.broadcast_to(accum_ref[m : m + 1, :], (128, 128)), 0.0
            )
            grown = jnp.dot(
                terms, ones, precision=lax.Precision.HIGHEST, preferred_element_type=F32
            )
            fresh[rows, :] = table_ref[rows, :] - learn_rate * row_grad / jnp.sqrt(grown)
            new_accum_ref[m : m + 1, :] = jnp.sum(
                jnp.where(diagonal, grown, 0.0), axis=0, keepdims=True
            )
        tables[n].start()
        towers[n].wait()
        weights[n].start()
    bias_ref[...] = tower_ref[pl.ds(columns, 1), :]
    for n in range(4):
        tables[n].wait()
        weights[n].wait()


def finish(total, tower, table, accum, columns):
    vmem = pltpu.VMEM
    return pl.pallas_call(
        finish_kernel,
        out_shape=(
            jax.ShapeDtypeStruct((columns, 128), F32),
            jax.ShapeDtypeStruct(table.shape, F32),
            jax.ShapeDtypeStruct(accum.shape, F32),
            jax.ShapeDtypeStruct((1, 128), F32),
        ),
        in_specs=[pl.BlockSpec(memory_space=pl.ANY)] * 2 + [pl.BlockSpec(memory_space=vmem)] * 2,
        out_specs=[pl.BlockSpec(memory_space=pl.ANY)] * 2 + [pl.BlockSpec(memory_space=vmem)] * 2,
        scratch_shapes=[
            vmem(table.shape, F32),
            vmem(table.shape, F32),
            vmem((columns + 8, 128), F32),
            pltpu.SemaphoreType.DMA((16,)),
        ],
        compiler_params=pltpu.CompilerParams(vmem_limit_bytes=58 << 20),
    )(total, tower, table, accum)


def step(pooled, upstream, preact, tower_w, ids, local_rows, dense, ny, nx):
    samples = upstream.shape[0]
    groups = ny * nx * 2
    nz = dense // 2
    batch = samples // groups
    columns = tower_w.shape[0]
    chunks = columns // CHUNK
    entries = ids.shape[1]
    slots = groups * CAP
    shard = -(-local_rows // (dense * 8)) * 8
    piece = -(-(columns + 8) // (nz * 32)) * 16
    turns = nz // 2
    vmem = pltpu.VMEM
    dma = pltpu.SemaphoreType.DMA
    total, tower = pl.pallas_call(
        functools.partial(step_kernel, ny, nx, nz, local_rows),
        out_shape=(
            jax.ShapeDtypeStruct((dense, shard, 128), F32),
            jax.ShapeDtypeStruct((nz * 2 * piece, 128), F32),
        ),
        in_specs=[pl.BlockSpec(memory_space=pl.ANY)] + [pl.BlockSpec(memory_space=vmem)] * 4,
        out_specs=[pl.BlockSpec(memory_space=vmem), pl.BlockSpec(memory_space=pl.ANY)],
        scratch_shapes=[
            vmem(pooled.shape, BF16),
            vmem((groups, batch, 128), F32),
            vmem((nx * ny, batch, 128), F32),
            vmem((nx * ny, batch, 128), F32),
            vmem((chunks, CHUNK, 128), F32),
            vmem((chunks, CHUNK, 128), F32),
            vmem((nx * ny * batch, 128), F32),
            vmem((2, nx * ny * batch, 256), BF16),
            vmem((chunks, CHUNK, 256), BF16),
            vmem((chunks, nx, ny * batch, CHUNK), F32),
            vmem((chunks, 2, 2 * batch, CHUNK), F32),
            vmem((chunks, 2, ny * batch, CHUNK), F32),
            vmem((chunks, 3, batch, CHUNK), F32),
            vmem((columns // 128, batch, 128), F32),
            vmem((slots, entries), BF16),
            vmem((groups, CAP, 128), F32),
            vmem((groups, CAP, 128), F32),
            vmem((8, slots), jnp.int32),
            vmem((nz, 2 * shard, slots), BF16),
            vmem((nz, 2 * shard, 128), F32),
            vmem((nz, shard, 128), F32),
            vmem((nz, shard, 128), F32),
            vmem((nz, shard, 128), F32),
            vmem((2, turns - turns // 2 + 1, shard, 128), F32),
            vmem((dense, shard, 128), F32),
            vmem((nz * 2 * piece, 128), F32),
            vmem((2, turns, 2, piece, 128), F32),
            vmem((2, piece, 128), F32),
            vmem((nz * 2 * piece, 128), F32),
            dma,
            dma,
            dma((chunks,)),
            dma((chunks,)),
            dma((4, chunks)),
            dma((4, chunks)),
            dma((3, chunks)),
            dma((3, chunks)),
            dma((groups,)),
            dma((groups,)),
        ]
        + [dma((nz,))] * 8
        + [
            dma((2, turns, 2)),
            dma((2, turns, 2)),
            dma((2,)),
            dma((2,)),
            dma((2, turns, 2)),
            dma((2, turns, 2)),
        ]
        + [dma((2, turns - turns // 2 + 1))] * 4
        + [dma, dma],
        compiler_params=pltpu.CompilerParams(
            collective_id=0, has_side_effects=True, vmem_limit_bytes=58 << 20
        ),
        cost_estimate=pl.CostEstimate(flops=1 << 30, bytes_accessed=8 << 20, transcendentals=0),
    )(pooled, upstream, preact, tower_w, ids)
    return total.reshape(dense * shard, 128), tower


def shards(pooled, upstream, preact, tower_w, row_ids, table, accum):
    groups = lax.axis_size("emb")
    dense = lax.axis_size("dense")
    local_rows = table.shape[0]
    ids = row_ids.reshape(groups, -1, row_ids.shape[1]).transpose(0, 2, 1).reshape(groups, -1)
    total, tower = step(
        pooled, upstream, preact, tower_w, ids, local_rows, dense, 4, 4
    )
    columns = tower_w.shape[0]
    weight_grad, new_table, new_accum, bias_grad = finish(
        total, tower, table, accum.reshape(-1, 128), columns
    )
    return (weight_grad, bias_grad.reshape(-1), new_table, new_accum.reshape(-1))


def solution(mesh):
    placed = (
        P("dense", None),
        P("dense", "emb"),
        P("dense", "emb"),
        P(None, "emb"),
        P("dense", None),
        P("emb", None),
        P("emb"),
    )
    return jax.shard_map(
        shards,
        mesh=mesh,
        in_specs=placed,
        out_specs=(P(None, "emb"), P("emb"), P("emb", None), P("emb")),
        check_vma=False,
    )
```
